128 devices in a mesh: dp: 8 (over x, core), dap: 16 (over y, z).
Axes of the slice: x: 4, y: 4, z: 4, core: 2. Of those that a mesh axis runs over, the one named last changes fastest.
Arguments:
- pair_act: bfloat16 [8, 256, 256, 128], P('dp', 'dap'), may hold values from -6 to 6
- cotangent: bfloat16 [8, 256, 256, 128], P('dp', 'dap'), may hold values from -6 to 6
- residue_mask: int32 [8, 256], P('dp'), may hold values 0 or 1
- weights: bfloat16 [4, 128, 128], replicated, may hold values from -0.5 to 0.5
- error_in: float32 [8, 4, 128, 128], P('dp'), may hold values from -6 to 6
- q_init: float32 [4, 128, 32], replicated, may hold values from -6 to 6
Outputs:
- grad_pair: bfloat16 [8, 256, 256, 128], P('dp', 'dap')
- update: float32 [4, 128, 128], replicated
- error_out: float32 [8, 4, 128, 128], P('dp')
The draws below stay inside these ranges and needn't reach their ends.
Inputs may be any that keep to these rules, and one draw needn't show every extreme that they name: `residue_mask`: 1 marks a present residue, 0 an absent one.
All inputs are finite; a program needn't handle non-finite values. No bound on the sum of `residue_mask` on one device may be relied on, other than what follows from the above.
Results may differ from the reference program's by a relative error of at most 0.02.
Values may be sent and summed in bfloat16 or wider, within the bound.
A program may use at most 192 MiB of HBM per device.

```python
import jax
import jax.numpy as jnp
from jax import lax

C = 128
RANK = 32
N = 256
CROPS = 8


def with_ends(drawn, own_key, smallest, largest):
    longest = drawn.shape.index(max(drawn.shape))
    spots = []
    for shift in (0, 1):
        where = [jax.random.randint(jax.random.fold_in(own_key, axis), (), 0, length) for axis, length in enumerate(drawn.shape)]
        where[longest] = (where[longest] + shift) % drawn.shape[longest]
        spots.append(tuple(where))
    return drawn.at[spots[0]].set(smallest).at[spots[1]].set(largest)


def level_of(stream_key, dims, split, least, top_value):
    loudness = 1.0
    for axis_at, shards_of in split:
        steps = jax.random.uniform(jax.random.fold_in(jax.random.fold_in(stream_key, 6), axis_at), (shards_of,), jnp.float32, least / len(split), top_value / len(split))
        loudness = loudness * jnp.repeat(jnp.exp(steps), dims[axis_at] // shards_of).reshape((-1,) + (1,) * (len(dims) - 1 - axis_at))
    return loudness


def noise(rng, extent, scale, limit, pieces=(), held_as=jnp.bfloat16):
    loudness = level_of(rng, extent, pieces, -0.22, 0.18) if pieces else 1.0
    drawn = jax.random.normal(rng, extent, jnp.float32) * scale * loudness
    return jnp.minimum(jnp.maximum(drawn, -limit), limit).astype(held_as)


def setup_inputs(seed: int = 0) -> dict:
    streams_of = jax.random.split(jax.random.key(seed), 7)
    pair_act = noise(streams_of[0], (CROPS, N, N, C), 1.0, 6.0, ((0, 8), (1, 16)))
    cotangent = noise(streams_of[1], (CROPS, N, N, C), 1.0, 6.0, ((0, 8), (1, 16)))
    residue_mask = with_ends((jax.random.randint(streams_of[2], (CROPS, N), 0, 8) < 7).astype(jnp.int32), jax.random.fold_in(streams_of[2], 1), 0, 1)
    weights = noise(streams_of[3], (4, C, C), C ** -0.5, 0.5)
    error_in = noise(streams_of[4], (CROPS, 4, C, C), 0.5, 6.0, ((0, 8),), jnp.float32)
    q_init = noise(streams_of[5], (4, C, RANK), 1.0, 6.0, (), jnp.float32)
    return dict(pair_act=pair_act, cotangent=cotangent, residue_mask=residue_mask, weights=weights, error_in=error_in, q_init=q_init)


EPS = 1e-05
HIGH = lax.Precision.HIGHEST

def layer_norm(values):
    centre = values - lax.optimization_barrier(jnp.mean(values, axis=-1, keepdims=True))
    inverse = lax.rsqrt(lax.optimization_barrier(jnp.mean(centre * centre, axis=-1, keepdims=True)) + EPS)
    return (centre * inverse, inverse)

def norm_back(upstream, normal, inverse):
    first = lax.optimization_barrier(jnp.mean(upstream, axis=-1, keepdims=True))
    second = lax.optimization_barrier(jnp.mean(upstream * normal, axis=-1, keepdims=True))
    return inverse * (upstream - first - normal * second)

def matmul(left_op, right_op):
    return jnp.dot(left_op, right_op, preferred_element_type=jnp.float32)

def flat_gram(left_op, right_op):
    width = left_op.shape[-1]
    return matmul(left_op.reshape(-1, width).T, right_op.reshape(-1, right_op.shape[-1]))

def orthonormal(panel):
    columns = []
    for column in range(panel.shape[1]):
        vector = panel[:, column]
        for basis_col in columns:
            vector = vector - jnp.dot(basis_col, vector, precision=HIGH) * basis_col
        columns.append(vector / jnp.sqrt(jnp.dot(vector, vector, precision=HIGH)))
    return jnp.stack(columns, axis=1)

def crop_backward(pair_tile, upstream, residue, weights):
    w_left, w_right, w_gate, w_out = (weights[0], weights[1], weights[2], weights[3])
    z_hat, z_inv = layer_norm(pair_tile.astype(jnp.float32))
    normed = z_hat.astype(jnp.bfloat16)
    keep = residue.astype(jnp.float32)
    pair_mask = (keep[:, None] * keep[None, :])[:, :, None]
    left_act = (pair_mask * matmul(normed, w_left)).astype(jnp.bfloat16)
    right_act = (pair_mask * matmul(normed, w_right)).astype(jnp.bfloat16)
    product = jnp.einsum('ikc,jkc->ijc', left_act.astype(jnp.float32), right_act.astype(jnp.float32))
    x_hat, x_inv = layer_norm(product)
    x_normed = x_hat.astype(jnp.bfloat16)
    gate = jax.nn.sigmoid(matmul(normed, w_gate))
    projected = matmul(x_normed, w_out)
    grad_up = upstream.astype(jnp.float32)
    grad_proj = (grad_up * gate).astype(jnp.bfloat16)
    grad_logit = (grad_up * projected * gate * (1.0 - gate)).astype(jnp.bfloat16)
    grad_prod = norm_back(matmul(grad_proj, w_out.T), x_hat, x_inv).astype(jnp.bfloat16)
    grad_left = jnp.einsum('ijc,jkc->ikc', grad_prod.astype(jnp.float32), right_act.astype(jnp.float32))
    grad_right = jnp.einsum('ijc,ikc->jkc', grad_prod.astype(jnp.float32), left_act.astype(jnp.float32))
    masked_left = (pair_mask * grad_left).astype(jnp.bfloat16)
    masked_right = (pair_mask * grad_right).astype(jnp.bfloat16)
    grad_normed = matmul(grad_logit, w_gate.T) + matmul(masked_left, w_left.T) + matmul(masked_right, w_right.T)
    grad_pair = norm_back(grad_normed, z_hat, z_inv).astype(jnp.bfloat16)
    count = pair_tile.shape[0]
    weight_grads = jnp.stack([flat_gram(normed, masked_left), flat_gram(normed, masked_right), flat_gram(normed, grad_logit), flat_gram(x_normed, grad_proj)]) / count
    return (grad_pair, weight_grads)

def reference(pair_act, cotangent, residue_mask, weights, error_in, q_init):

    def one_crop(items):
        return crop_backward(items[0], items[1], items[2], weights)
    grad_pair, crop_grads = lax.map(one_crop, (pair_act, cotangent, residue_mask))
    replicas = pair_act.shape[0]
    memory = crop_grads + error_in
    panel = jnp.einsum('rwcd,wde->wce', memory, q_init, precision=HIGH) / replicas
    basis = jax.vmap(orthonormal)(panel)
    coeffs = jnp.einsum('rwcd,wce->wde', memory, basis, precision=HIGH) / replicas
    update = jnp.einsum('wce,wde->wcd', basis, coeffs, precision=HIGH)
    return (grad_pair, update, memory - update[None])
```

```python
import functools

import jax
import jax.numpy as jnp
from jax import lax
from jax.experimental import pallas as pl
from jax.experimental.pallas import tpu as pltpu
from jax.sharding import PartitionSpec as P

EPS = 1e-05
HIGH = lax.Precision.HIGHEST
MESH = pl.DeviceIdType.MESH
F32 = jnp.float32
BF16 = jnp.bfloat16
C = 128
N = 256
ROWS = 16
SLICE = 8
PITCH = 17
RANK = 32
DAP = 16
DP = 8
OFFSETS = sorted(
    [(dy, dz) for dy in range(4) for dz in range(4) if (dy, dz) != (0, 0)],
    key=lambda o: min(o[0], 4 - o[0]) + min(o[1], 4 - o[1]),
)


def nn(a, b):
    return lax.dot_general(a, b, (((1,), (0,)), ((), ())), preferred_element_type=F32)


def nt(a, b):
    return lax.dot_general(a, b, (((1,), (1,)), ((), ())), preferred_element_type=F32)


def tn(a, b):
    return lax.dot_general(a, b, (((0,), (0,)), ((), ())), preferred_element_type=F32)


def peers():
    me = lax.axis_index("dap")
    y, z = me // 4, lax.rem(me, 4)
    sign = 1 - 2 * lax.rem(lax.axis_index("dp"), 2)
    return [
        lax.rem(y + sign * dy + 4, 4) * 4 + lax.rem(z + sign * dz + 4, 4)
        for dy, dz in OFFSETS
    ]


def dap_barrier():
    me = lax.axis_index("dap")
    barrier = pltpu.get_barrier_semaphore()
    for step in range(1, DAP):
        pl.semaphore_signal(
            barrier, inc=1, device_id={"dap": lax.rem(me + step, DAP)}, device_id_type=MESH
        )
    pl.semaphore_wait(barrier, DAP - 1)


def to_channels(src, dst, half, send, recv, own):
    me = lax.axis_index("dap")
    lanes = pl.ds(half * 128, 128)
    rows = pl.ds(pl.multiple_of(me * ROWS, ROWS), ROWS)
    copies = []
    for t, peer in enumerate(peers()):
        copy = pltpu.make_async_remote_copy(
            src_ref=src.at[pl.ds(peer * SLICE, SLICE), :, lanes],
            dst_ref=dst.at[:, rows, lanes],
            send_sem=send.at[half, t],
            recv_sem=recv.at[half, t],
            device_id={"dap": peer},
            device_id_type=MESH,
        )
        copy.start()
        copies.append(copy)
    local = pltpu.make_async_copy(
        src.at[pl.ds(me * SLICE, SLICE), :, lanes], dst.at[:, rows, lanes], own.at[half]
    )
    local.start()
    return copies, local


def to_rows(src, dst, half, send, recv, own):
    me = lax.axis_index("dap")
    lanes = pl.ds(half * 128, 128)
    channels = pl.ds(me * SLICE, SLICE)
    copies = []
    for t, peer in enumerate(peers()):
        copy = pltpu.make_async_remote_copy(
            src_ref=src.at[:, pl.ds(pl.multiple_of(peer * ROWS, ROWS), ROWS), lanes],
            dst_ref=dst.at[channels, :, lanes],
            send_sem=send.at[half, t],
            recv_sem=recv.at[half, t],
            device_id={"dap": peer},
            device_id_type=MESH,
        )
        copy.start()
        copies.append(copy)
    local = pltpu.make_async_copy(
        src.at[:, pl.ds(pl.multiple_of(me * ROWS, ROWS), ROWS), lanes],
        dst.at[channels, :, lanes],
        own.at[half],
    )
    local.start()
    return copies, local


def arrive(started):
    copies, local = started
    for copy in copies:
        copy.wait_recv()
    local.wait()


def sent(started):
    for copy in started[0]:
        copy.wait_send()


def set_up(residue, weights, mask, lr_t, lr):
    me = lax.axis_index("dap")
    keep = residue[...].astype(F32)
    col = lax.broadcasted_iota(jnp.int32, (ROWS, N), 1)
    row = lax.broadcasted_iota(jnp.int32, (ROWS, N), 0) + me * ROWS
    keep_rows = jnp.sum(jnp.where(col == row, keep, 0.0), axis=1, keepdims=True)
    mask[...] = keep_rows * keep
    for w in range(2):
        lr_t[w * C : (w + 1) * C, :] = weights[w].astype(F32).T.astype(BF16)
        lr[:, w * C : (w + 1) * C] = weights[w]


def front(pair, lr_t, normed, z_hat, z_inv, tall):
    def step(i, _):
        x = pair[i].astype(F32)
        centre = x - jnp.sum(x, axis=-1, keepdims=True) * (1.0 / C)
        inv = lax.rsqrt(jnp.sum(centre * centre, axis=-1, keepdims=True) * (1.0 / C) + EPS)
        z = centre * inv
        nb = z.astype(BF16)
        normed[i] = nb
        z_hat[i] = z
        z_inv[i] = jnp.broadcast_to(inv, (N, C))
        both = nt(lr_t[...], nb)
        for w in range(2):
            for half in range(2):
                tall.at[w, half][pl.ds(i, C, stride=PITCH), :] = both[
                    w * C : (w + 1) * C, half * 128 : (half + 1) * 128
                ]
        return 0

    lax.fori_loop(0, ROWS, step, 0, unroll=2)


def pack(tall, w, half, mask, dst):
    m = mask[:, half * 128 : (half + 1) * 128]

    def step(b, _):
        for u in range(8):
            tile = tall[w, half, pl.ds(b * 8 * PITCH + u * PITCH, ROWS), :]
            dst[b * 8 + u, :, half * 128 : (half + 1) * 128] = (tile * m).astype(BF16)
        return 0

    lax.fori_loop(0, C // 8, step, 0)


def first_triangle(left, right, prod):
    def step(c, _):
        prod[c] = nt(left[c], right[c]).astype(BF16)
        return 0

    lax.fori_loop(0, SLICE, step, 0, unroll=2)


def mid_norm(x, half, tall, x_inv):
    lanes = slice(half * 128, (half + 1) * 128)

    def total(b, acc):
        for u in range(8):
            acc = acc + x[b * 8 + u, :, lanes].astype(F32)
        return acc

    mean = lax.fori_loop(0, C // 8, total, jnp.zeros((ROWS, 128), F32)) * (1.0 / C)

    def square(b, acc):
        for u in range(8):
            d = x[b * 8 + u, :, lanes].astype(F32) - mean
            acc = acc + d * d
        return acc

    var = lax.fori_loop(0, C // 8, square, jnp.zeros((ROWS, 128), F32)) * (1.0 / C)
    inv = lax.rsqrt(var + EPS)
    x_inv[:, lanes] = inv

    def store(b, _):
        for u in range(8):
            v = (x[b * 8 + u, :, lanes].astype(F32) - mean) * inv
            tall[0, half, pl.ds(b * 8 * PITCH + u * PITCH, ROWS), :] = v
        return 0

    lax.fori_loop(0, C // 8, store, 0)


def mid_mix(half, cot, normed, weights, tall, from_gate, grads):
    lanes = slice(half * 128, (half + 1) * 128)

    def step(i, carry):
        gate_grad, out_grad = carry
        xn = tall.at[0, half][pl.ds(i, C, stride=PITCH), :].astype(BF16)
        nb = normed[i, lanes, :]
        gate = jax.nn.sigmoid(nn(nb, weights[2]))
        projected = tn(xn, weights[3])
        up = cot[i, lanes, :].astype(F32)
        grad_proj = (up * gate).astype(BF16)
        grad_logit = (up * projected * gate * (1.0 - gate)).astype(BF16)
        gate_grad = gate_grad + tn(nb, grad_logit)
        out_grad = out_grad + nn(xn, grad_proj)
        tall.at[1, half][pl.ds(i, C, stride=PITCH), :] = nt(weights[3], grad_proj)
        from_gate[i, lanes, :] = nt(grad_logit, weights[2])
        return gate_grad, out_grad

    zero = jnp.zeros((C, C), F32)
    gate_grad, out_grad = lax.fori_loop(0, ROWS, step, (zero, zero), unroll=2)
    if half == 0:
        grads[2] = gate_grad
        grads[3] = out_grad
    else:
        grads[2] = grads[2] + gate_grad
        grads[3] = grads[3] + out_grad


def mid_back(half, tall, x_inv, dst):
    lanes = slice(half * 128, (half + 1) * 128)

    def total(b, acc):
        first, second = acc
        for u in range(8):
            at = pl.ds(b * 8 * PITCH + u * PITCH, ROWS)
            h = tall[1, half, at, :]
            first = first + h
            second = second + h * tall[0, half, at, :]
        return first, second

    zero = jnp.zeros((ROWS, 128), F32)
    first, second = lax.fori_loop(0, C // 8, total, (zero, zero))
    first = first * (1.0 / C)
    second = second * (1.0 / C)
    inv = x_inv[:, lanes]

    def store(b, _):
        for u in range(8):
            at = pl.ds(b * 8 * PITCH + u * PITCH, ROWS)
            v = inv * (tall[1, half, at, :] - first - tall[0, half, at, :] * second)
            dst[b * 8 + u, :, lanes] = v.astype(BF16)
        return 0

    lax.fori_loop(0, C // 8, store, 0)


def second_triangle(grad, left, right, to_left, to_right):
    def step(c, _):
        g = grad[c]
        to_left[c] = nn(g, right[c]).astype(BF16)
        to_right[c] = tn(g, left[c]).astype(BF16)
        return 0

    lax.fori_loop(0, SLICE, step, 0, unroll=2)


def unpack(src, w, half, mask, tall):
    lanes = slice(half * 128, (half + 1) * 128)
    m = mask[:, lanes]

    def step(b, _):
        for u in range(8):
            tall[w, half, pl.ds(b * 8 * PITCH + u * PITCH, ROWS), :] = (
                src[b * 8 + u, :, lanes].astype(F32) * m
            )
        return 0

    lax.fori_loop(0, C // 8, step, 0)


def last(half, tall, normed, z_hat, z_inv, from_gate, lr, out, grads):
    lanes = slice(half * 128, (half + 1) * 128)

    def step(i, acc):
        parts = [tall.at[w, half][pl.ds(i, C, stride=PITCH), :].astype(BF16) for w in range(2)]
        both = jnp.concatenate(parts, axis=0)
        acc = acc + nn(both, normed[i, lanes, :])
        grad = nn(lr[...], both).T + from_gate[i, lanes, :]
        z = z_hat[i, lanes, :]
        first = jnp.sum(grad, axis=-1, keepdims=True) * (1.0 / C)
        second = jnp.sum(grad * z, axis=-1, keepdims=True) * (1.0 / C)
        out[i, lanes, :] = (z_inv[i, lanes, :] * (grad - first - z * second)).astype(BF16)
        return acc

    acc = lax.fori_loop(0, ROWS, step, jnp.zeros((2 * C, C), F32), unroll=2)
    for w in range(2):
        if half == 0:
            grads[w] = acc[w * C : (w + 1) * C].T
        else:
            grads[w] = grads[w] + acc[w * C : (w + 1) * C].T


def main_kernel(
    pair, cot, residue, weights, out, grads,
    mask, lr_t, lr, normed, z_hat, z_inv, from_gate, x_inv, tall,
    send_l, send_r, left, right, prod, x, send_g, grad, to_l, to_r, got_l, got_r,
    send, recv, own,
):
    dap_barrier()
    set_up(residue, weights, mask, lr_t, lr)
    front(pair, lr_t, normed, z_hat, z_inv, tall)
    started = []
    for half in range(2):
        for w, (src, dst) in enumerate([(send_l, left), (send_r, right)]):
            pack(tall, w, half, mask, src)
            started.append(to_channels(src, dst, half, send.at[w], recv.at[w], own.at[w]))
    for s in started:
        arrive(s)
    first_triangle(left, right, prod)
    back = [to_rows(prod, x, half, send.at[2], recv.at[2], own.at[2]) for half in range(2)]
    again = []
    for half in range(2):
        arrive(back[half])
        mid_norm(x, half, tall, x_inv)
        mid_mix(half, cot, normed, weights, tall, from_gate, grads)
        mid_back(half, tall, x_inv, send_g)
        again.append(to_channels(send_g, grad, half, send.at[3], recv.at[3], own.at[3]))
    for s in again:
        arrive(s)
    second_triangle(grad, left, right, to_l, to_r)
    ends = []
    for half in range(2):
        for w, (src, dst) in enumerate([(to_l, got_l), (to_r, got_r)]):
            ends.append(to_rows(src, dst, half, send.at[4 + w], recv.at[4 + w], own.at[4 + w]))
    for half in range(2):
        for w, src in enumerate([got_l, got_r]):
            arrive(ends[2 * half + w])
            unpack(src, w, half, mask, tall)
        last(half, tall, normed, z_hat, z_inv, from_gate, lr, out, grads)
    for s in started + back + again + ends:
        sent(s)


def main_call(pair, cot, residue, weights):
    vmem = pl.BlockSpec(memory_space=pltpu.VMEM)
    by_rows = pltpu.VMEM((C, ROWS, N), BF16)
    by_channels = pltpu.VMEM((SLICE, N, N), BF16)
    wide = pltpu.VMEM((ROWS, N, C), F32)
    return pl.pallas_call(
        main_kernel,
        name="triangle",
        out_shape=(
            jax.ShapeDtypeStruct((ROWS, N, C), BF16),
            jax.ShapeDtypeStruct((4, C, C), F32),
        ),
        in_specs=[vmem] * 4,
        out_specs=(vmem, vmem),
        scratch_shapes=[
            pltpu.VMEM((ROWS, N), F32),
            pltpu.VMEM((2 * C, C), BF16),
            pltpu.VMEM((C, 2 * C), BF16),
            pltpu.VMEM((ROWS, N, C), BF16),
            wide,
            wide,
            wide,
            pltpu.VMEM((ROWS, N), F32),
            pltpu.VMEM((2, 2, C * PITCH, 128), F32),
            by_rows, by_rows, by_channels, by_channels,
            by_channels, by_rows,
            by_rows, by_channels,
            by_channels, by_channels, by_rows, by_rows,
            pltpu.SemaphoreType.DMA((6, 2, DAP - 1)),
            pltpu.SemaphoreType.DMA((6, 2, DAP - 1)),
            pltpu.SemaphoreType.DMA((6, 2)),
        ],
        compiler_params=pltpu.CompilerParams(
            collective_id=0, has_side_effects=True, vmem_limit_bytes=56 << 20
        ),
    )(pair, cot, residue, weights)


def orthonormal(panel):
    columns = []
    for column in range(panel.shape[1]):
        vector = panel[:, column]
        for basis_col in columns:
            vector = vector - jnp.dot(basis_col, vector, precision=HIGH) * basis_col
        columns.append(vector / jnp.sqrt(jnp.dot(vector, vector, precision=HIGH)))
    return jnp.stack(columns, axis=1)


def per_device(pair_act, cotangent, residue_mask, weights, error_in, q_init):
    replicas = lax.axis_size("dp")
    grad_pair, local_grads = main_call(pair_act[0], cotangent[0], residue_mask, weights)
    crop_grads = lax.psum(local_grads.astype(BF16), "dap").astype(F32) / N
    memory = crop_grads + error_in[0]
    local_panel = jnp.einsum("wcd,wde->wce", memory, q_init, precision=HIGH)
    panel = lax.psum(local_panel, "dp") / replicas
    basis = jax.vmap(orthonormal)(panel)
    local_coeffs = jnp.einsum("wcd,wce->wde", memory, basis, precision=HIGH)
    coeffs = lax.psum(local_coeffs.astype(jnp.bfloat16), "dp").astype(jnp.float32) / replicas
    update = jnp.einsum("wce,wde->wcd", basis, coeffs, precision=HIGH)
    return (grad_pair[None], update, (memory - update)[None])


def solution(mesh):
    placed = (
        P("dp", "dap", None, None),
        P("dp", "dap", None, None),
        P("dp", None),
        P(),
        P("dp", None, None, None),
        P(),
    )
    return jax.shard_map(
        per_device,
        mesh=mesh,
        in_specs=placed,
        out_specs=(P("dp", "dap", None, None), P(), P("dp", None, None, None)),
        check_vma=False,
    )
```

```python
import functools

import jax
import jax.numpy as jnp
from jax import lax
from jax.experimental import pallas as pl
from jax.experimental.pallas import tpu as pltpu
from jax.sharding import PartitionSpec as P

EPS = 1e-05
HIGH = lax.Precision.HIGHEST
MESH = pl.DeviceIdType.MESH
F32 = jnp.float32
BF16 = jnp.bfloat16
C = 128
N = 256
ROWS = 16
SLICE = 8
PITCH = 17
RANK = 32
DAP = 16
DP = 8
OFFSETS = sorted(
    [(dy, dz) for dy in range(4) for dz in range(4) if (dy, dz) != (0, 0)],
    key=lambda o: min(o[0], 4 - o[0]) + min(o[1], 4 - o[1]),
)


def nn(a, b):
    return lax.dot_general(a, b, (((1,), (0,)), ((), ())), preferred_element_type=F32)


def nt(a, b):
    return lax.dot_general(a, b, (((1,), (1,)), ((), ())), preferred_element_type=F32)


def tn(a, b):
    return lax.dot_general(a, b, (((0,), (0,)), ((), ())), preferred_element_type=F32)


def peers():
    me = lax.axis_index("dap")
    y, z = me // 4, lax.rem(me, 4)
    sign = 1 - 2 * lax.rem(lax.axis_index("dp"), 2)
    return [
        lax.rem(y + sign * dy + 4, 4) * 4 + lax.rem(z + sign * dz + 4, 4)
        for dy, dz in OFFSETS
    ]


def greet():
    barrier = pltpu.get_barrier_semaphore()
    for axis, size in (("dap", DAP), ("dp", DP)):
        me = lax.axis_index(axis)
        for step in range(1, size):
            pl.semaphore_signal(
                barrier, inc=1, device_id={axis: lax.rem(me + step, size)}, device_id_type=MESH
            )


def greeted():
    pl.semaphore_wait(pltpu.get_barrier_semaphore(), DAP + DP - 2)


def remote(src, dst, send, recv, axis, peer):
    copy = pltpu.make_async_remote_copy(
        src_ref=src, dst_ref=dst, send_sem=send, recv_sem=recv,
        device_id={axis: peer}, device_id_type=MESH,
    )
    copy.start()
    return copy


def exchange(src, dst, half, send, recv):
    me = lax.axis_index("dap")
    for peer in peers():
        remote(src.at[half, peer], dst.at[half, me], send.at[half], recv.at[half], "dap", peer)
    pltpu.make_async_copy(src.at[half, me], dst.at[half, me], recv.at[half]).start()


def await_bytes(ref, sem):
    pltpu.make_async_copy(ref, ref, sem).wait()


def set_up(residue, weights, mask, lr_t, lr):
    me = lax.axis_index("dap")
    keep = residue[...].astype(F32)
    col = lax.broadcasted_iota(jnp.int32, (ROWS, N), 1)
    row = lax.broadcasted_iota(jnp.int32, (ROWS, N), 0) + me * ROWS
    keep_rows = jnp.sum(jnp.where(col == row, keep, 0.0), axis=1, keepdims=True)
    mask[...] = keep_rows * keep
    for w in range(2):
        lr_t[w * C : (w + 1) * C, :] = weights[w].astype(F32).T.astype(BF16)
        lr[:, w * C : (w + 1) * C] = weights[w]


def front(half, pair, lr_t, normed, z_hat, z_inv, tall):
    lanes = slice(half * 128, (half + 1) * 128)

    def step(i, _):
        x = pair[i, lanes, :].astype(F32)
        centre = x - jnp.sum(x, axis=-1, keepdims=True) * (1.0 / C)
        inv = lax.rsqrt(jnp.sum(centre * centre, axis=-1, keepdims=True) * (1.0 / C) + EPS)
        z = centre * inv
        nb = z.astype(BF16)
        normed[i, lanes, :] = nb
        z_hat[i, lanes, :] = z
        z_inv[i, lanes, :] = jnp.broadcast_to(inv, (128, C))
        both = nt(lr_t[...], nb)
        for w in range(2):
            tall.at[w, half][pl.ds(i, C, stride=PITCH), :] = both[w * C : (w + 1) * C]
        return 0

    lax.fori_loop(0, ROWS, step, 0, unroll=4)


def tile_at(b, u):
    return pl.ds(b * SLICE * PITCH + u * PITCH, ROWS)


def pack(tall, w, half, mask, dst):
    m = mask[:, half * 128 : (half + 1) * 128]

    def step(b, _):
        for u in range(SLICE):
            dst[half, b, u] = (tall[w, half, tile_at(b, u), :] * m).astype(BF16)
        return 0

    lax.fori_loop(0, DAP, step, 0)


def plane(ref, half, c):
    return ref[half, :, c].reshape(N, 128)


def whole(ref, c):
    return jnp.concatenate([plane(ref, 0, c), plane(ref, 1, c)], axis=1)


def first_triangle(half, left, right, prod):
    def step(c, _):
        cols = right[:, half * DAP // 2 : (half + 1) * DAP // 2, c]
        cols = jnp.concatenate([cols[0].reshape(128, 128), cols[1].reshape(128, 128)], axis=1)
        prod[half, :, c] = nt(whole(left, c), cols).astype(BF16).reshape(DAP, ROWS, 128)
        return 0

    lax.fori_loop(0, SLICE, step, 0, unroll=4)


def mid_norm(x, half, tall, x_inv):
    lanes = slice(half * 128, (half + 1) * 128)
    zero = jnp.zeros((ROWS, 128), F32)

    def total(b, acc):
        for u in range(SLICE):
            acc = acc + x[half, b, u].astype(F32)
        return acc

    mean = lax.fori_loop(0, DAP, total, zero) * (1.0 / C)

    def square(b, acc):
        for u in range(SLICE):
            d = x[half, b, u].astype(F32) - mean
            acc = acc + d * d
        return acc

    var = lax.fori_loop(0, DAP, square, zero) * (1.0 / C)
    inv = lax.rsqrt(var + EPS)
    x_inv[:, lanes] = inv

    def store(b, _):
        for u in range(SLICE):
            tall[0, half, tile_at(b, u), :] = (x[half, b, u].astype(F32) - mean) * inv
        return 0

    lax.fori_loop(0, DAP, store, 0)


def mid_mix(half, cot, normed, weights, tall, from_gate, grads):
    lanes = slice(half * 128, (half + 1) * 128)

    def step(i, carry):
        gate_grad, out_grad = carry
        xn = tall.at[0, half][pl.ds(i, C, stride=PITCH), :].astype(BF16)
        nb = normed[i, lanes, :]
        gate = jax.nn.sigmoid(nn(nb, weights[2]))
        projected = tn(xn, weights[3])
        up = cot[i, lanes, :].astype(F32)
        grad_proj = (up * gate).astype(BF16)
        grad_logit = (up * projected * gate * (1.0 - gate)).astype(BF16)
        gate_grad = gate_grad + tn(nb, grad_logit)
        out_grad = out_grad + nn(xn, grad_proj)
        tall.at[1, half][pl.ds(i, C, stride=PITCH), :] = nt(weights[3], grad_proj)
        from_gate[i, lanes, :] = nt(grad_logit, weights[2])
        return gate_grad, out_grad

    zero = jnp.zeros((C, C), F32)
    gate_grad, out_grad = lax.fori_loop(0, ROWS, step, (zero, zero), unroll=2)
    if half == 0:
        grads[2] = gate_grad
        grads[3] = out_grad
    else:
        grads[2] = grads[2] + gate_grad
        grads[3] = grads[3] + out_grad


def mid_back(half, tall, x_inv, dst):
    lanes = slice(half * 128, (half + 1) * 128)

    def total(b, acc):
        first, second = acc
        for u in range(SLICE):
            h = tall[1, half, tile_at(b, u), :]
            first = first + h
            second = second + h * tall[0, half, tile_at(b, u), :]
        return first, second

    zero = jnp.zeros((ROWS, 128), F32)
    first, second = lax.fori_loop(0, DAP, total, (zero, zero))
    first = first * (1.0 / C)
    second = second * (1.0 / C)
    inv = x_inv[:, lanes]

    def store(b, _):
        for u in range(SLICE):
            at = tile_at(b, u)
            v = inv * (tall[1, half, at, :] - first - tall[0, half, at, :] * second)
            dst[half, b, u] = v.astype(BF16)
        return 0

    lax.fori_loop(0, DAP, store, 0)


def grad_of_left(half, grad, right, dst):
    def step(c, _):
        dst[half, :, c] = nn(whole(grad, c), plane(right, half, c)).astype(BF16).reshape(DAP, ROWS, 128)
        return 0

    lax.fori_loop(0, SLICE, step, 0, unroll=4)


def grad_of_right(half, grad, left, dst):
    def step(c, _):
        dst[half, :, c] = tn(whole(grad, c), plane(left, half, c)).astype(BF16).reshape(DAP, ROWS, 128)
        return 0

    lax.fori_loop(0, SLICE, step, 0, unroll=4)


def unpack(src, w, half, mask, tall):
    m = mask[:, half * 128 : (half + 1) * 128]

    def step(b, _):
        for u in range(SLICE):
            tall[w, half, tile_at(b, u), :] = src[half, b, u].astype(F32) * m
        return 0

    lax.fori_loop(0, DAP, step, 0)


def both_sides(half, i, tall):
    return jnp.concatenate(
        [tall.at[w, half][pl.ds(i, C, stride=PITCH), :].astype(BF16) for w in range(2)], axis=0
    )


def last_grads(half, tall, normed, both, grads):
    lanes = slice(half * 128, (half + 1) * 128)

    def step(i, acc):
        pair = both_sides(half, i, tall)
        both[i] = pair
        return acc + nn(pair, normed[i, lanes, :])

    acc = lax.fori_loop(0, ROWS, step, jnp.zeros((2 * C, C), F32), unroll=4)
    for w in range(2):
        new = acc[w * C : (w + 1) * C].T
        grads[w] = new if half == 0 else grads[w] + new


def last_pair(half, both, z_hat, z_inv, from_gate, lr, out):
    lanes = slice(half * 128, (half + 1) * 128)

    def step(i, _):
        grad = nn(lr[...], both[i]).T + from_gate[i, lanes, :]
        z = z_hat[i, lanes, :]
        first = jnp.sum(grad, axis=-1, keepdims=True) * (1.0 / C)
        second = jnp.sum(grad * z, axis=-1, keepdims=True) * (1.0 / C)
        out[i, lanes, :] = (z_inv[i, lanes, :] * (grad - first - z * second)).astype(BF16)
        return 0

    lax.fori_loop(0, ROWS, step, 0, unroll=4)


def gram_schmidt(panel):
    row = lax.broadcasted_iota(jnp.int32, (8, 1), 0)
    for j in range(RANK):
        at, sub = j // 8, j % 8
        for tiles in panel:
            v = jnp.broadcast_to(tiles[at][sub : sub + 1, :], (8, C))
            dots = [
                jnp.sum(tiles[t] * v, axis=1, keepdims=True) if t >= at else None
                for t in range(RANK // 8)
            ]
            scale = 1.0 / jnp.broadcast_to(dots[at][sub : sub + 1, :], (8, 1))
            for t in range(at, RANK // 8):
                coef = dots[t] * scale
                if t == at:
                    coef = jnp.where(row > sub, coef, 0.0)
                tiles[t] = tiles[t] - coef * v
    return [
        jnp.concatenate(
            [t * lax.rsqrt(jnp.sum(t * t, axis=1, keepdims=True)) for t in tiles], axis=0
        )
        for tiles in panel
    ]


def compress(grads, error_in, q_init, update, error_out, bufs, sems, meanwhile):
    part16, got16, crop16, chunk, got32, mean = bufs
    send, recv = sems
    me, dp = lax.axis_index("dap"), lax.axis_index("dp")
    rows = 4 * C // DAP
    mine = pl.ds(pl.multiple_of(me * rows, rows), rows)
    others = peers()

    for w in range(4):
        part16[w * C : (w + 1) * C, :] = grads[w].astype(BF16)
    for t, peer in enumerate(others):
        block = part16.at[pl.ds(pl.multiple_of(peer * rows, rows), rows)]
        remote(block, got16.at[t], send.at[0], recv.at[0], "dap", peer)
    meanwhile()
    await_bytes(got16, recv.at[0])
    total = part16[mine, :].astype(F32)
    for t in range(DAP - 1):
        total = total + got16[t].astype(F32)
    crop16[mine, :] = (total * (1.0 / N)).astype(BF16)

    matrix, first = me // 4, pl.multiple_of(lax.rem(me, 4) * rows, rows)
    chunk[...] = crop16[mine, :].astype(F32) + error_in[matrix, pl.ds(first, rows), :]
    got32[dp] = chunk[...]
    for s in range(1, DP):
        remote(chunk, got32.at[dp], send.at[1], recv.at[1], "dp", lax.rem(dp + s, DP))
    for peer in others:
        remote(crop16.at[mine], crop16.at[mine], send.at[2], recv.at[2], "dap", peer)
    await_bytes(got32.at[pl.ds(0, DP - 1)], recv.at[1])
    total = got32[0]
    for r in range(1, DP):
        total = total + got32[r]
    mean[mine, :] = total * (1.0 / DP)
    for peer in others:
        remote(mean.at[mine], mean.at[mine], send.at[3], recv.at[3], "dap", peer)
    gathered = pl.ds(0, 4 * C - rows)
    await_bytes(mean.at[gathered], recv.at[3])

    panel = []
    for w in range(4):
        rows_of = lax.dot_general(
            q_init[w], mean[w * C : (w + 1) * C, :], (((1,), (1,)), ((), ())),
            preferred_element_type=F32, precision=HIGH,
        )
        panel.append([rows_of[t * 8 : (t + 1) * 8, :] for t in range(RANK // 8)])
    basis = gram_schmidt(panel)
    await_bytes(crop16.at[gathered], recv.at[2])
    for w in range(4):
        here = slice(w * C, (w + 1) * C)
        coeffs = lax.dot_general(
            basis[w], mean[here, :], (((1,), (0,)), ((), ())),
            preferred_element_type=F32, precision=HIGH,
        )
        new = lax.dot_general(
            basis[w], coeffs, (((0,), (0,)), ((), ())),
            preferred_element_type=F32, precision=HIGH,
        )
        update[w] = new
        error_out[w] = crop16[here, :].astype(F32) + error_in[w] - new
    await_bytes(part16.at[gathered], send.at[0])
    await_bytes(got32.at[pl.ds(0, DP - 1)], send.at[1])
    await_bytes(crop16.at[gathered], send.at[2])
    await_bytes(mean.at[gathered], send.at[3])


def main_kernel(
    pair_in, cot_in, error_at, q_at, residue, weights, out, update, error_out,
    pair, cot, error_in, q_init,
    grads, mask, lr_t, lr, normed, z_hat, z_inv, from_gate, x_inv, tall, both,
    send_l, send_r, left, right, prod, x, send_g, grad, to_l, to_r, got_l, got_r,
    part16, got16, crop16, chunk, got32, mean,
    fetch, send, recv, send_c, recv_c,
):
    fetched = []
    for k, (src, dst) in enumerate(
        [
            (pair_in.at[:, pl.ds(0, 128)], pair.at[:, pl.ds(0, 128)]),
            (pair_in.at[:, pl.ds(128, 128)], pair.at[:, pl.ds(128, 128)]),
            (cot_in, cot),
            (error_at, error_in),
            (q_at, q_init),
        ]
    ):
        copy = pltpu.make_async_copy(src, dst, fetch.at[k])
        copy.start()
        fetched.append(copy)
    greet()
    set_up(residue, weights, mask, lr_t, lr)
    started = []

    def begin(k, half, src, dst):
        exchange(src, dst, half, send.at[k], recv.at[k])
        started.append((src, half, k))

    def arrive(k, half, dst):
        await_bytes(dst.at[half], recv.at[k, half])

    sides = [(send_l, left), (send_r, right)]
    for half in range(2):
        fetched[half].wait()
        front(half, pair, lr_t, normed, z_hat, z_inv, tall)
        for w, (src, dst) in enumerate(sides):
            pack(tall, w, half, mask, src)
            if half == 0 and w == 0:
                greeted()
            begin(w, half, src, dst)
    for copy in fetched[2:]:
        copy.wait()
    for half in range(2):
        for w in range(2):
            arrive(w, half, sides[w][1])
    for half in range(2):
        first_triangle(half, left, right, prod)
        begin(2, half, prod, x)
    for half in range(2):
        arrive(2, half, x)
        mid_norm(x, half, tall, x_inv)
        mid_mix(half, cot, normed, weights, tall, from_gate, grads)
        mid_back(half, tall, x_inv, send_g)
        begin(3, half, send_g, grad)
    for half in range(2):
        arrive(3, half, grad)
    for half in range(2):
        grad_of_left(half, grad, right, to_l)
        begin(4, half, to_l, got_l)
        grad_of_right(half, grad, left, to_r)
        begin(5, half, to_r, got_r)
    for half in range(2):
        for w, src in enumerate([got_l, got_r]):
            arrive(4 + w, half, src)
            unpack(src, w, half, mask, tall)
        last_grads(half, tall, normed, both, grads)
        if half == 0:
            last_pair(half, both, z_hat, z_inv, from_gate, lr, out)
    compress(
        grads, error_in, q_init, update, error_out,
        (part16, got16, crop16, chunk, got32, mean), (send_c, recv_c),
        lambda: last_pair(1, both, z_hat, z_inv, from_gate, lr, out),
    )
    for src, half, k in started:
        await_bytes(src.at[half, pl.ds(0, DAP - 1)], send.at[k, half])


def main_call(*operands):
    vmem = pl.BlockSpec(memory_space=pltpu.VMEM)
    hbm = pl.BlockSpec(memory_space=pl.ANY)
    blocks = pltpu.VMEM((2, DAP, SLICE, ROWS, 128), BF16)
    wide = pltpu.VMEM((ROWS, N, C), F32)
    half_wide = pltpu.VMEM((ROWS, N, C), BF16)
    part = 4 * C // DAP
    return pl.pallas_call(
        main_kernel,
        name="triangle",
        out_shape=(
            pltpu.VMEM((ROWS, N, C), BF16),
            pltpu.VMEM((4, C, C), F32),
            pltpu.VMEM((4, C, C), F32),
        ),
        in_specs=[hbm] * 4 + [vmem] * 2,
        out_specs=(vmem, vmem, vmem),
        scratch_shapes=[
            half_wide,
            half_wide,
            pltpu.VMEM((4, C, C), F32),
            pltpu.VMEM((4, RANK, C), F32),
            pltpu.VMEM((4, C, C), F32),
            pltpu.VMEM((ROWS, N), F32),
            pltpu.VMEM((2 * C, C), BF16),
            pltpu.VMEM((C, 2 * C), BF16),
            half_wide,
            wide,
            wide,
            wide,
            pltpu.VMEM((ROWS, N), F32),
            pltpu.VMEM((2, 2, C * PITCH, 128), F32),
            pltpu.VMEM((ROWS, 2 * C, 128), BF16),
        ]
        + [blocks] * 12
        + [
            pltpu.VMEM((4 * C, C), BF16),
            pltpu.VMEM((DAP - 1, part, C), BF16),
            pltpu.VMEM((4 * C, C), BF16),
            pltpu.VMEM((part, C), F32),
            pltpu.VMEM((DP, part, C), F32),
            pltpu.VMEM((4 * C, C), F32),
            pltpu.SemaphoreType.DMA((5,)),
            pltpu.SemaphoreType.DMA((6, 2)),
            pltpu.SemaphoreType.DMA((6, 2)),
            pltpu.SemaphoreType.DMA((4,)),
            pltpu.SemaphoreType.DMA((4,)),
        ],
        compiler_params=pltpu.CompilerParams(
            collective_id=0, has_side_effects=True, vmem_limit_bytes=56 << 20
        ),
    )(*operands)


def store_kernel(*refs):
    sources, targets, sems = refs[:3], refs[3:6], refs[6]
    copies = [
        pltpu.make_async_copy(src, dst, sems.at[k])
        for k, (src, dst) in enumerate(zip(sources, targets))
    ]
    for copy in copies:
        copy.start()
    for copy in copies:
        copy.wait()


def store(*arrays):
    vmem = pl.BlockSpec(memory_space=pltpu.VMEM)
    hbm = pl.BlockSpec(memory_space=pl.ANY)
    return pl.pallas_call(
        store_kernel,
        name="store",
        out_shape=tuple(jax.ShapeDtypeStruct(a.shape, a.dtype) for a in arrays),
        in_specs=[vmem] * 3,
        out_specs=(hbm,) * 3,
        scratch_shapes=[pltpu.SemaphoreType.DMA((3,))],
        compiler_params=pltpu.CompilerParams(vmem_limit_bytes=8 << 20),
    )(*arrays)


def per_device(pair_act, cotangent, residue_mask, weights, error_in, q_init):
    results = main_call(
        pair_act[0], cotangent[0], error_in[0], q_init.transpose(0, 2, 1), residue_mask, weights
    )
    grad_pair, update, error_out = store(*results)
    return (grad_pair[None], update, error_out[None])


def solution(mesh):
    placed = (
        P("dp", "dap", None, None),
        P("dp", "dap", None, None),
        P("dp", None),
        P(),
        P("dp", None, None, None),
        P(),
    )
    return jax.shard_map(
        per_device,
        mesh=mesh,
        in_specs=placed,
        out_specs=(P("dp", "dap", None, None), P(), P("dp", None, None, None)),
        check_vma=False,
    )
```

```python
import functools

import jax
import jax.numpy as jnp
from jax import lax
from jax.experimental import pallas as pl
from jax.experimental.pallas import tpu as pltpu
from jax.sharding import PartitionSpec as P

EPS = 1e-05
HIGH = lax.Precision.HIGHEST
MESH = pl.DeviceIdType.MESH
F32 = jnp.float32
BF16 = jnp.bfloat16
C = 128
N = 256
ROWS = 16
SLICE = 8
PITCH = 17
RANK = 32
DAP = 16
DP = 8
OFFSETS = [(2,2),(1,2),(3,2),(2,1),(2,3),(1,1),(3,3),(1,3),(3,1),(2,0),(0,2),(1,0),(3,0),(0,1),(0,3)]


def nn(a, b):
    return lax.dot_general(a, b, (((1,), (0,)), ((), ())), preferred_element_type=F32)


def nt(a, b):
    return lax.dot_general(a, b, (((1,), (1,)), ((), ())), preferred_element_type=F32)


def tn(a, b):
    return lax.dot_general(a, b, (((0,), (0,)), ((), ())), preferred_element_type=F32)


def peers():
    me = lax.axis_index("dap")
    y, z = me // 4, lax.rem(me, 4)
    sign = 1 - 2 * lax.rem(lax.axis_index("dp"), 2)
    return [
        lax.rem(y + sign * dy + 4, 4) * 4 + lax.rem(z + sign * dz + 4, 4)
        for dy, dz in OFFSETS
    ]


def greet():
    barrier = pltpu.get_barrier_semaphore()
    for axis, size in (("dap", DAP), ("dp", DP)):
        me = lax.axis_index(axis)
        for step in range(1, size):
            pl.semaphore_signal(
                barrier, inc=1, device_id={axis: lax.rem(me + step, size)}, device_id_type=MESH
            )


def greeted():
    pl.semaphore_wait(pltpu.get_barrier_semaphore(), DAP + DP - 2)


def remote(src, dst, send, recv, axis, peer):
    copy = pltpu.make_async_remote_copy(
        src_ref=src, dst_ref=dst, send_sem=send, recv_sem=recv,
        device_id={axis: peer}, device_id_type=MESH,
    )
    copy.start()
    return copy


def exchange(src, dst, half, send, recv):
    me = lax.axis_index("dap")
    for peer in peers():
        remote(src.at[half, peer], dst.at[half, me], send.at[half], recv.at[half], "dap", peer)
    pltpu.make_async_copy(src.at[half, me], dst.at[half, me], recv.at[half]).start()


def await_bytes(ref, sem):
    pltpu.make_async_copy(ref, ref, sem).wait()


def set_up(residue, weights, mask, lr_t, lr, gate_t):
    me = lax.axis_index("dap")
    keep = residue[...].astype(F32)
    col = lax.broadcasted_iota(jnp.int32, (ROWS, N), 1)
    row = lax.broadcasted_iota(jnp.int32, (ROWS, N), 0) + me * ROWS
    keep_rows = jnp.sum(jnp.where(col == row, keep, 0.0), axis=1, keepdims=True)
    mask[...] = keep_rows * keep
    for w in range(2):
        lr_t[w * C : (w + 1) * C, :] = weights[w].astype(F32).T.astype(BF16)
        lr[:, w * C : (w + 1) * C] = weights[w]
    gate_t[...] = weights[2].astype(F32).T.astype(BF16)


def front(half, pair, lr_t, normed, normed_t, z_hat, z_inv, tall):
    lanes = slice(half * 128, (half + 1) * 128)

    def step(i, _):
        x = pair[i, lanes, :].astype(F32)
        centre = x - jnp.sum(x, axis=-1, keepdims=True) * (1.0 / C)
        inv = lax.rsqrt(jnp.sum(centre * centre, axis=-1, keepdims=True) * (1.0 / C) + EPS)
        z = centre * inv
        nb = z.astype(BF16)
        nb_t = nb.T
        normed[i, lanes, :] = nb
        normed_t[half, i] = nb_t
        z_hat[i, lanes, :] = z
        z_inv[i, lanes, :] = jnp.broadcast_to(inv, (128, C))
        both = nn(lr_t[...], nb_t)
        for w in range(2):
            tall.at[w, half][pl.ds(i, C, stride=PITCH), :] = both[w * C : (w + 1) * C]
        return 0

    lax.fori_loop(0, ROWS, step, 0, unroll=4)


def gating(half, cot, normed, weights, gate, grad_proj, tall, h_mean):
    lanes = slice(half * 128, (half + 1) * 128)

    def step(i, _):
        g = jax.nn.sigmoid(nn(normed[i, lanes, :], weights[2]))
        gp = (cot[i, lanes, :].astype(F32) * g).astype(BF16)
        gate[i, lanes, :] = g
        grad_proj[i, lanes, :] = gp
        tall.at[1, half][pl.ds(i, C, stride=PITCH), :] = nt(weights[3], gp)
        return 0

    lax.fori_loop(0, ROWS, step, 0, unroll=4)

    def total(b, acc):
        for u in range(SLICE):
            acc = acc + tall[1, half, tile_at(b, u), :]
        return acc

    zero = jnp.zeros((ROWS, 128), F32)
    h_mean[:, lanes] = lax.fori_loop(0, DAP, total, zero) * (1.0 / C)


def tile_at(b, u):
    return pl.ds(b * SLICE * PITCH + u * PITCH, ROWS)


def pack(tall, w, half, mask, dst):
    m = mask[:, half * 128 : (half + 1) * 128]

    def step(b, _):
        for u in range(SLICE):
            dst[half, b, u] = (tall[w, half, tile_at(b, u), :] * m).astype(BF16)
        return 0

    lax.fori_loop(0, DAP, step, 0)


def plane(ref, half, c):
    return ref[half, :, c].reshape(N, 128)


def whole(ref, c):
    return jnp.concatenate([plane(ref, 0, c), plane(ref, 1, c)], axis=1)


def first_triangle(half, left, right, prod):
    def step(c, _):
        cols = right[:, half * DAP // 2 : (half + 1) * DAP // 2, c]
        cols = jnp.concatenate([cols[0].reshape(128, 128), cols[1].reshape(128, 128)], axis=1)
        prod[half, :, c] = nt(whole(left, c), cols).astype(BF16).reshape(DAP, ROWS, 128)
        return 0

    lax.fori_loop(0, SLICE, step, 0, unroll=4)


def mid_core(half, x, tall, h_mean, x_mean, x_inv, dst):
    lanes = slice(half * 128, (half + 1) * 128)
    zero = jnp.zeros((ROWS, 128), F32)

    def total(b, acc):
        for u in range(SLICE):
            acc = acc + x[half, b, u].astype(F32)
        return acc

    mean = lax.fori_loop(0, DAP, total, zero) * (1.0 / C)

    def square(b, acc):
        squares, dots = acc
        for u in range(SLICE):
            d = x[half, b, u].astype(F32) - mean
            squares = squares + d * d
            dots = dots + d * tall[1, half, tile_at(b, u), :]
        return squares, dots

    squares, dots = lax.fori_loop(0, DAP, square, (zero, zero))
    inv = lax.rsqrt(squares * (1.0 / C) + EPS)
    second = dots * inv * (1.0 / C)
    first = h_mean[:, lanes]
    x_mean[:, lanes] = mean
    x_inv[:, lanes] = inv

    def store(b, _):
        for u in range(SLICE):
            x_hat = (x[half, b, u].astype(F32) - mean) * inv
            v = inv * (tall[1, half, tile_at(b, u), :] - first - x_hat * second)
            dst[half, b, u] = v.astype(BF16)
        return 0

    lax.fori_loop(0, DAP, store, 0)


def mid_rest(half, x, x_mean, x_inv, cot, normed_t, gate, grad_proj, weights, gate_t, tall, from_gate, grads):
    lanes = slice(half * 128, (half + 1) * 128)
    mean = x_mean[:, lanes]
    inv = x_inv[:, lanes]

    def store(b, _):
        for u in range(SLICE):
            tall[0, half, tile_at(b, u), :] = (x[half, b, u].astype(F32) - mean) * inv
        return 0

    lax.fori_loop(0, DAP, store, 0)

    def step(i, carry):
        gate_grad, out_grad = carry
        xn = tall.at[0, half][pl.ds(i, C, stride=PITCH), :].astype(BF16)
        projected = tn(xn, weights[3])
        g = gate[i, lanes, :]
        up = cot[i, lanes, :].astype(F32)
        grad_logit = (up * projected * g * (1.0 - g)).astype(BF16)
        from_gate[i, lanes, :] = nn(grad_logit, gate_t[...])
        gate_grad = gate_grad + nn(normed_t[half, i], grad_logit)
        out_grad = out_grad + nn(xn, grad_proj[i, lanes, :])
        return gate_grad, out_grad

    zero = jnp.zeros((C, C), F32)
    new = lax.fori_loop(0, ROWS, step, (zero, zero), unroll=4)
    for w in range(2):
        grads[2 + w] = new[w] if half == 0 else grads[2 + w] + new[w]


def grad_of_left(half, grad, right, dst):
    def step(c, _):
        dst[half, :, c] = nn(whole(grad, c), plane(right, half, c)).astype(BF16).reshape(DAP, ROWS, 128)
        return 0

    lax.fori_loop(0, SLICE, step, 0, unroll=4)


def grad_of_right(half, grad, left, dst):
    def step(c, _):
        dst[half, :, c] = tn(whole(grad, c), plane(left, half, c)).astype(BF16).reshape(DAP, ROWS, 128)
        return 0

    lax.fori_loop(0, SLICE, step, 0, unroll=4)


def unpack(src, w, half, mask, tall):
    m = mask[:, half * 128 : (half + 1) * 128]

    def step(b, _):
        for u in range(SLICE):
            tall[w, half, tile_at(b, u), :] = src[half, b, u].astype(F32) * m
        return 0

    lax.fori_loop(0, DAP, step, 0)


def last_grads(half, w, tall, normed, both, grads):
    lanes = slice(half * 128, (half + 1) * 128)
    rows = slice(w * C, (w + 1) * C)

    def step(i, acc):
        side = tall.at[w, half][pl.ds(i, C, stride=PITCH), :].astype(BF16)
        both[i, rows, :] = side
        return acc + nn(side, normed[i, lanes, :])

    acc = lax.fori_loop(0, ROWS, step, jnp.zeros((C, C), F32), unroll=8).T
    grads[w] = acc if half == 0 else grads[w] + acc


def last_pair(half, both, z_hat, z_inv, from_gate, lr, out):
    lanes = slice(half * 128, (half + 1) * 128)

    def step(i, _):
        grad = nn(lr[...], both[i]).T + from_gate[i, lanes, :]
        z = z_hat[i, lanes, :]
        first = jnp.sum(grad, axis=-1, keepdims=True) * (1.0 / C)
        second = jnp.sum(grad * z, axis=-1, keepdims=True) * (1.0 / C)
        out[i, lanes, :] = (z_inv[i, lanes, :] * (grad - first - z * second)).astype(BF16)
        return 0

    lax.fori_loop(0, ROWS, step, 0, unroll=4)


def gram_schmidt(panel):
    row = lax.broadcasted_iota(jnp.int32, (8, 1), 0)
    for j in range(RANK):
        at, sub = j // 8, j % 8
        for tiles in panel:
            v = jnp.broadcast_to(tiles[at][sub : sub + 1, :], (8, C))
            dots = [
                jnp.sum(tiles[t] * v, axis=1, keepdims=True) if t >= at else None
                for t in range(RANK // 8)
            ]
            scale = 1.0 / jnp.broadcast_to(dots[at][sub : sub + 1, :], (8, 1))
            for t in range(at, RANK // 8):
                coef = dots[t] * scale
                if t == at:
                    coef = jnp.where(row > sub, coef, 0.0)
                tiles[t] = tiles[t] - coef * v
    return [
        jnp.concatenate(
            [t * lax.rsqrt(jnp.sum(t * t, axis=1, keepdims=True)) for t in tiles], axis=0
        )
        for tiles in panel
    ]


def compress(grads, error_in, q_init, update, error_out, bufs, sems, meanwhile):
    part16, got16, crop16, chunk, got32, mean = bufs
    send, recv = sems
    me, dp = lax.axis_index("dap"), lax.axis_index("dp")
    rows = 4 * C // DAP
    mine = pl.ds(pl.multiple_of(me * rows, rows), rows)
    others = peers()

    for w in range(4):
        part16[w * C : (w + 1) * C, :] = grads[w].astype(BF16)
    for t, peer in enumerate(others):
        block = part16.at[pl.ds(pl.multiple_of(peer * rows, rows), rows)]
        remote(block, got16.at[t], send.at[0], recv.at[0], "dap", peer)
    meanwhile()
    await_bytes(got16, recv.at[0])
    total = part16[mine, :].astype(F32)
    for t in range(DAP - 1):
        total = total + got16[t].astype(F32)
    crop16[mine, :] = (total * (1.0 / N)).astype(BF16)

    matrix, first = me // 4, pl.multiple_of(lax.rem(me, 4) * rows, rows)
    chunk[...] = crop16[mine, :].astype(F32) + error_in[matrix, pl.ds(first, rows), :]
    got32[dp] = chunk[...]
    for s in range(1, DP):
        remote(chunk, got32.at[dp], send.at[1], recv.at[1], "dp", lax.rem(dp + s, DP))
    for peer in others:
        remote(crop16.at[mine], crop16.at[mine], send.at[2], recv.at[2], "dap", peer)
    await_bytes(got32.at[pl.ds(0, DP - 1)], recv.at[1])
    total = got32[0]
    for r in range(1, DP):
        total = total + got32[r]
    mean[mine, :] = total * (1.0 / DP)
    for peer in others:
        remote(mean.at[mine], mean.at[mine], send.at[3], recv.at[3], "dap", peer)
    gathered = pl.ds(0, 4 * C - rows)
    await_bytes(mean.at[gathered], recv.at[3])

    panel = []
    for w in range(4):
        rows_of = lax.dot_general(
            q_init[w], mean[w * C : (w + 1) * C, :], (((1,), (1,)), ((), ())),
            preferred_element_type=F32, precision=HIGH,
        )
        panel.append([rows_of[t * 8 : (t + 1) * 8, :] for t in range(RANK // 8)])
    basis = gram_schmidt(panel)
    await_bytes(crop16.at[gathered], recv.at[2])
    for w in range(4):
        here = slice(w * C, (w + 1) * C)
        coeffs = lax.dot_general(
            basis[w], mean[here, :], (((1,), (0,)), ((), ())),
            preferred_element_type=F32, precision=HIGH,
        )
        new = lax.dot_general(
            basis[w], coeffs, (((0,), (0,)), ((), ())),
            preferred_element_type=F32, precision=HIGH,
        )
        update[w] = new
        error_out[w] = crop16[here, :].astype(F32) + error_in[w] - new
    await_bytes(part16.at[gathered], send.at[0])
    await_bytes(got32.at[pl.ds(0, DP - 1)], send.at[1])
    await_bytes(crop16.at[gathered], send.at[2])
    await_bytes(mean.at[gathered], send.at[3])


def main_kernel(
    pair_in, cot_in, error_at, q_at, residue, weights, out, update, error_out,
    pair, cot, error_in, q_init,
    grads, mask, lr_t, lr, gate_t, normed, normed_t, gate, grad_proj, z_hat, z_inv, from_gate,
    h_mean, x_mean, x_inv, tall, both,
    send_l, send_r, left, right, prod, x, send_g, grad, to_l, to_r, got_l, got_r,
    part16, got16, crop16, chunk, got32, mean,
    fetch, send, recv, send_c, recv_c,
):
    fetched = []
    for k, (src, dst) in enumerate(
        [
            (pair_in.at[:, pl.ds(0, 128)], pair.at[:, pl.ds(0, 128)]),
            (pair_in.at[:, pl.ds(128, 128)], pair.at[:, pl.ds(128, 128)]),
            (cot_in, cot),
            (error_at, error_in),
            (q_at, q_init),
        ]
    ):
        copy = pltpu.make_async_copy(src, dst, fetch.at[k])
        copy.start()
        fetched.append(copy)
    greet()
    set_up(residue, weights, mask, lr_t, lr, gate_t)
    started = []

    def begin(k, half, src, dst):
        exchange(src, dst, half, send.at[k], recv.at[k])
        started.append((src, half, k))

    def arrive(k, half, dst):
        await_bytes(dst.at[half], recv.at[k, half])

    sides = [(send_l, left), (send_r, right)]
    for half in range(2):
        fetched[half].wait()
        front(half, pair, lr_t, normed, normed_t, z_hat, z_inv, tall)
        for w, (src, dst) in enumerate(sides):
            pack(tall, w, half, mask, src)
            if half == 0 and w == 0:
                greeted()
            begin(w, half, src, dst)
    for copy in fetched[2:]:
        copy.wait()
    for half in range(2):
        gating(half, cot, normed, weights, gate, grad_proj, tall, h_mean)
    for half in range(2):
        for w in range(2):
            arrive(w, half, sides[w][1])
    for half in range(2):
        first_triangle(half, left, right, prod)
        begin(2, half, prod, x)
    for half in range(2):
        arrive(2, half, x)
        mid_core(half, x, tall, h_mean, x_mean, x_inv, send_g)
        begin(3, half, send_g, grad)
        mid_rest(
            half, x, x_mean, x_inv, cot, normed_t, gate, grad_proj, weights, gate_t,
            tall, from_gate, grads,
        )
    for half in range(2):
        arrive(3, half, grad)
    for half in range(2):
        grad_of_left(half, grad, right, to_l)
        begin(4, half, to_l, got_l)
        grad_of_right(half, grad, left, to_r)
        begin(5, half, to_r, got_r)
    for half in range(2):
        for w, src in enumerate([got_l, got_r]):
            arrive(4 + w, half, src)
            unpack(src, w, half, mask, tall)
            last_grads(half, w, tall, normed, both, grads)
        if half == 0:
            last_pair(half, both, z_hat, z_inv, from_gate, lr, out)
    compress(
        grads, error_in, q_init, update, error_out,
        (part16, got16, crop16, chunk, got32, mean), (send_c, recv_c),
        lambda: last_pair(1, both, z_hat, z_inv, from_gate, lr, out),
    )
    for src, half, k in started:
        await_bytes(src.at[half, pl.ds(0, DAP - 1)], send.at[k, half])


def main_call(*operands):
    vmem = pl.BlockSpec(memory_space=pltpu.VMEM)
    hbm = pl.BlockSpec(memory_space=pl.ANY)
    blocks = pltpu.VMEM((2, DAP, SLICE, ROWS, 128), BF16)
    wide = pltpu.VMEM((ROWS, N, C), F32)
    half_wide = pltpu.VMEM((ROWS, N, C), BF16)
    part = 4 * C // DAP
    return pl.pallas_call(
        main_kernel,
        name="triangle",
        out_shape=(
            pltpu.VMEM((ROWS, N, C), BF16),
            pltpu.VMEM((4, C, C), F32),
            pltpu.VMEM((4, C, C), F32),
        ),
        in_specs=[hbm] * 4 + [vmem] * 2,
        out_specs=(vmem, vmem, vmem),
        scratch_shapes=[
            half_wide,
            half_wide,
            pltpu.VMEM((4, C, C), F32),
            pltpu.VMEM((4, RANK, C), F32),
            pltpu.VMEM((4, C, C), F32),
            pltpu.VMEM((ROWS, N), F32),
            pltpu.VMEM((2 * C, C), BF16),
            pltpu.VMEM((C, 2 * C), BF16),
            pltpu.VMEM((C, C), BF16),
            half_wide,
            pltpu.VMEM((2, ROWS, C, 128), BF16),
            wide,
            half_wide,
            wide,
            wide,
            wide,
            pltpu.VMEM((ROWS, N), F32),
            pltpu.VMEM((ROWS, N), F32),
            pltpu.VMEM((ROWS, N), F32),
            pltpu.VMEM((2, 2, C * PITCH, 128), F32),
            pltpu.VMEM((ROWS, 2 * C, 128), BF16),
        ]
        + [blocks] * 12
        + [
            pltpu.VMEM((4 * C, C), BF16),
            pltpu.VMEM((DAP - 1, part, C), BF16),
            pltpu.VMEM((4 * C, C), BF16),
            pltpu.VMEM((part, C), F32),
            pltpu.VMEM((DP, part, C), F32),
            pltpu.VMEM((4 * C, C), F32),
            pltpu.SemaphoreType.DMA((5,)),
            pltpu.SemaphoreType.DMA((6, 2)),
            pltpu.SemaphoreType.DMA((6, 2)),
            pltpu.SemaphoreType.DMA((4,)),
            pltpu.SemaphoreType.DMA((4,)),
        ],
        compiler_params=pltpu.CompilerParams(
            collective_id=0, has_side_effects=True, vmem_limit_bytes=56 << 20
        ),
    )(*operands)


def store_kernel(*refs):
    sources, targets, sems = refs[:3], refs[3:6], refs[6]
    copies = [
        pltpu.make_async_copy(src, dst, sems.at[k])
        for k, (src, dst) in enumerate(zip(sources, targets))
    ]
    for copy in copies:
        copy.start()
    for copy in copies:
        copy.wait()


def store(*arrays):
    vmem = pl.BlockSpec(memory_space=pltpu.VMEM)
    hbm = pl.BlockSpec(memory_space=pl.ANY)
    return pl.pallas_call(
        store_kernel,
        name="store",
        out_shape=tuple(jax.ShapeDtypeStruct(a.shape, a.dtype) for a in arrays),
        in_specs=[vmem] * 3,
        out_specs=(hbm,) * 3,
        scratch_shapes=[pltpu.SemaphoreType.DMA((3,))],
        compiler_params=pltpu.CompilerParams(vmem_limit_bytes=8 << 20),
    )(*arrays)


def per_device(pair_act, cotangent, residue_mask, weights, error_in, q_init):
    results = main_call(
        pair_act[0], cotangent[0], error_in[0], q_init.transpose(0, 2, 1), residue_mask, weights
    )
    grad_pair, update, error_out = store(*results)
    return (grad_pair[None], update, error_out[None])


def solution(mesh):
    placed = (
        P("dp", "dap", None, None),
        P("dp", "dap", None, None),
        P("dp", None),
        P(),
        P("dp", None, None, None),
        P(),
    )
    return jax.shard_map(
        per_device,
        mesh=mesh,
        in_specs=placed,
        out_specs=(P("dp", "dap", None, None), P(), P("dp", None, None, None)),
        check_vma=False,
    )
```

```python
import functools

import jax
import jax.numpy as jnp
from jax import lax
from jax.experimental import pallas as pl
from jax.experimental.pallas import tpu as pltpu
from jax.sharding import PartitionSpec as P

EPS = 1e-05
HIGH = lax.Precision.HIGHEST
MESH = pl.DeviceIdType.MESH
F32 = jnp.float32
BF16 = jnp.bfloat16
C = 128
N = 256
ROWS = 16
SLICE = 8
GROUP = 4
PITCH = 17
RANK = 32
DAP = 16
DP = 8
PART = 2 * C // DAP
OFFSETS = [(2,2),(1,2),(3,2),(2,1),(2,3),(1,1),(3,3),(1,3),(3,1),(2,0),(0,2),(1,0),(3,0),(0,1),(0,3)]


def nn(a, b):
    return lax.dot_general(a, b, (((1,), (0,)), ((), ())), preferred_element_type=F32)


def nt(a, b):
    return lax.dot_general(a, b, (((1,), (1,)), ((), ())), preferred_element_type=F32)


def exact(a, b, a_dim, b_dim):
    dims = (((a_dim,), (b_dim,)), ((), ()))
    return lax.dot_general(a, b, dims, preferred_element_type=F32, precision=HIGH)


def tn(a, b):
    return lax.dot_general(a, b, (((0,), (0,)), ((), ())), preferred_element_type=F32)


def peers():
    me = lax.axis_index("dap")
    y, z = me // 4, lax.rem(me, 4)
    sign = 1 - 2 * lax.rem(lax.axis_index("dp"), 2)
    return [
        lax.rem(y + sign * dy + 4, 4) * 4 + lax.rem(z + sign * dz + 4, 4)
        for dy, dz in OFFSETS
    ]


def greet():
    barrier = pltpu.get_barrier_semaphore()
    for axis, size in (("dap", DAP), ("dp", DP)):
        me = lax.axis_index(axis)
        for step in range(1, size):
            pl.semaphore_signal(
                barrier, inc=1, device_id={axis: lax.rem(me + step, size)}, device_id_type=MESH
            )


def greeted():
    pl.semaphore_wait(pltpu.get_barrier_semaphore(), DAP + DP - 2)


def remote(src, dst, send, recv, axis, peer):
    copy = pltpu.make_async_remote_copy(
        src_ref=src, dst_ref=dst, send_sem=send, recv_sem=recv,
        device_id={axis: peer}, device_id_type=MESH,
    )
    copy.start()
    return copy


def exchange(src, dst, half, group, send, recv):
    me = lax.axis_index("dap")
    these = pl.ds(group * GROUP, GROUP)
    for peer in peers():
        remote(
            src.at[half, peer, these], dst.at[half, me, these],
            send.at[half], recv.at[half, group], "dap", peer,
        )
    pltpu.make_async_copy(src.at[half, me, these], dst.at[half, me, these], recv.at[half, group]).start()


def await_bytes(ref, sem):
    pltpu.make_async_copy(ref, ref, sem).wait()


def set_up(residue, weights, mask, lr_t, lr, gate_t):
    me = lax.axis_index("dap")
    keep = residue[...].astype(F32)
    col = lax.broadcasted_iota(jnp.int32, (ROWS, N), 1)
    row = lax.broadcasted_iota(jnp.int32, (ROWS, N), 0) + me * ROWS
    keep_rows = jnp.sum(jnp.where(col == row, keep, 0.0), axis=1, keepdims=True)
    mask[...] = keep_rows * keep
    for w in range(2):
        lr_t[w * C : (w + 1) * C, :] = weights[w].astype(F32).T.astype(BF16)
        lr[:, w * C : (w + 1) * C] = weights[w]
    gate_t[...] = weights[2].astype(F32).T.astype(BF16)


def front(half, pair, lr_t, normed, normed_t, z_hat, z_inv, tall):
    lanes = slice(half * 128, (half + 1) * 128)

    def step(i, _):
        x = pair[i, lanes, :].astype(F32)
        centre = x - jnp.sum(x, axis=-1, keepdims=True) * (1.0 / C)
        inv = lax.rsqrt(jnp.sum(centre * centre, axis=-1, keepdims=True) * (1.0 / C) + EPS)
        z = centre * inv
        nb = z.astype(BF16)
        nb_t = nb.T
        normed[i, lanes, :] = nb
        normed_t[half, i] = nb_t
        z_hat[i, lanes, :] = z
        z_inv[i, lanes, :] = jnp.broadcast_to(inv, (128, C))
        both = nn(lr_t[...], nb_t)
        for w in range(2):
            tall.at[w, half][pl.ds(i, C, stride=PITCH), :] = both[w * C : (w + 1) * C]
        return 0

    lax.fori_loop(0, ROWS, step, 0, unroll=4)


def gating(half, cot, normed, weights, gate, grad_proj, tall, h_mean):
    lanes = slice(half * 128, (half + 1) * 128)

    def step(i, _):
        g = jax.nn.sigmoid(nn(normed[i, lanes, :], weights[2]))
        gp = (cot[i, lanes, :].astype(F32) * g).astype(BF16)
        gate[i, lanes, :] = g
        grad_proj[i, lanes, :] = gp
        tall.at[1, half][pl.ds(i, C, stride=PITCH), :] = nt(weights[3], gp)
        return 0

    lax.fori_loop(0, ROWS, step, 0, unroll=4)

    def total(b, acc):
        for u in range(SLICE):
            acc = acc + tall[1, half, tile_at(b, u), :]
        return acc

    zero = jnp.zeros((ROWS, 128), F32)
    h_mean[:, lanes] = lax.fori_loop(0, DAP, total, zero) * (1.0 / C)


def tile_at(b, u):
    return pl.ds(b * SLICE * PITCH + u * PITCH, ROWS)


def pack(tall, w, half, mask, dst):
    m = mask[:, half * 128 : (half + 1) * 128]

    def step(b, _):
        for u in range(SLICE):
            dst[half, b, u] = (tall[w, half, tile_at(b, u), :] * m).astype(BF16)
        return 0

    lax.fori_loop(0, DAP, step, 0)


def plane(ref, half, c):
    return ref[half, :, c].reshape(N, 128)


def whole(ref, c):
    return jnp.concatenate([plane(ref, 0, c), plane(ref, 1, c)], axis=1)


def first_triangle(half, group, left, right, prod):
    def step(c, _):
        cols = right[:, half * DAP // 2 : (half + 1) * DAP // 2, c]
        cols = jnp.concatenate([cols[0].reshape(128, 128), cols[1].reshape(128, 128)], axis=1)
        prod[half, :, c] = nt(whole(left, c), cols).astype(BF16).reshape(DAP, ROWS, 128)
        return 0

    lax.fori_loop(group * GROUP, (group + 1) * GROUP, step, 0, unroll=4)


def mid_core(half, x, tall, h_mean, x_mean, x_inv, dst):
    lanes = slice(half * 128, (half + 1) * 128)
    zero = jnp.zeros((ROWS, 128), F32)

    def total(b, acc):
        for u in range(SLICE):
            acc = acc + x[half, b, u].astype(F32)
        return acc

    mean = lax.fori_loop(0, DAP, total, zero) * (1.0 / C)

    def square(b, acc):
        squares, dots = acc
        for u in range(SLICE):
            d = x[half, b, u].astype(F32) - mean
            squares = squares + d * d
            dots = dots + d * tall[1, half, tile_at(b, u), :]
        return squares, dots

    squares, dots = lax.fori_loop(0, DAP, square, (zero, zero))
    inv = lax.rsqrt(squares * (1.0 / C) + EPS)
    second = dots * inv * (1.0 / C)
    first = h_mean[:, lanes]
    x_mean[:, lanes] = mean
    x_inv[:, lanes] = inv

    def store(b, _):
        for u in range(SLICE):
            x_hat = (x[half, b, u].astype(F32) - mean) * inv
            v = inv * (tall[1, half, tile_at(b, u), :] - first - x_hat * second)
            dst[half, b, u] = v.astype(BF16)
        return 0

    lax.fori_loop(0, DAP, store, 0)


def mid_rest(half, x, x_mean, x_inv, cot, normed_t, gate, grad_proj, weights, gate_t, tall, from_gate, grads):
    lanes = slice(half * 128, (half + 1) * 128)
    mean = x_mean[:, lanes]
    inv = x_inv[:, lanes]

    def store(b, _):
        for u in range(SLICE):
            tall[0, half, tile_at(b, u), :] = (x[half, b, u].astype(F32) - mean) * inv
        return 0

    lax.fori_loop(0, DAP, store, 0)

    def step(i, carry):
        gate_grad, out_grad = carry
        xn = tall.at[0, half][pl.ds(i, C, stride=PITCH), :].astype(BF16)
        projected = tn(xn, weights[3])
        g = gate[i, lanes, :]
        up = cot[i, lanes, :].astype(F32)
        grad_logit = (up * projected * g * (1.0 - g)).astype(BF16)
        from_gate[i, lanes, :] = nn(grad_logit, gate_t[...])
        gate_grad = gate_grad + nn(normed_t[half, i], grad_logit)
        out_grad = out_grad + nn(xn, grad_proj[i, lanes, :])
        return gate_grad, out_grad

    zero = jnp.zeros((C, C), F32)
    new = lax.fori_loop(0, ROWS, step, (zero, zero), unroll=4)
    for w in range(2):
        grads[2 + w] = new[w] if half == 0 else grads[2 + w] + new[w]


def grad_of_left(half, group, grad, right, dst):
    def step(c, _):
        dst[half, :, c] = nn(whole(grad, c), plane(right, half, c)).astype(BF16).reshape(DAP, ROWS, 128)
        return 0

    lax.fori_loop(group * GROUP, (group + 1) * GROUP, step, 0, unroll=4)


def grad_of_right(half, group, grad, left, dst):
    def step(c, _):
        dst[half, :, c] = tn(whole(grad, c), plane(left, half, c)).astype(BF16).reshape(DAP, ROWS, 128)
        return 0

    lax.fori_loop(group * GROUP, (group + 1) * GROUP, step, 0, unroll=4)


def unpack(src, w, half, mask, tall):
    m = mask[:, half * 128 : (half + 1) * 128]

    def step(b, _):
        for u in range(SLICE):
            tall[w, half, tile_at(b, u), :] = src[half, b, u].astype(F32) * m
        return 0

    lax.fori_loop(0, DAP, step, 0)


def last_grads(half, w, tall, normed, both, grads):
    lanes = slice(half * 128, (half + 1) * 128)
    rows = slice(w * C, (w + 1) * C)

    def step(i, acc):
        side = tall.at[w, half][pl.ds(i, C, stride=PITCH), :].astype(BF16)
        both[i, rows, :] = side
        return acc + nn(side, normed[i, lanes, :])

    acc = lax.fori_loop(0, ROWS, step, jnp.zeros((C, C), F32), unroll=8).T
    grads[w] = acc if half == 0 else grads[w] + acc


def last_pair(half, both, z_hat, z_inv, from_gate, lr, out):
    lanes = slice(half * 128, (half + 1) * 128)

    def step(i, _):
        grad = nn(lr[...], both[i]).T + from_gate[i, lanes, :]
        z = z_hat[i, lanes, :]
        first = jnp.sum(grad, axis=-1, keepdims=True) * (1.0 / C)
        second = jnp.sum(grad * z, axis=-1, keepdims=True) * (1.0 / C)
        out[i, lanes, :] = (z_inv[i, lanes, :] * (grad - first - z * second)).astype(BF16)
        return 0

    lax.fori_loop(0, ROWS, step, 0, unroll=4)


def gram_schmidt(panel):
    row = lax.broadcasted_iota(jnp.int32, (8, 1), 0)
    for j in range(RANK):
        at, sub = j // 8, j % 8
        for tiles in panel:
            v = jnp.broadcast_to(tiles[at][sub : sub + 1, :], (8, C))
            dots = [
                jnp.sum(tiles[t] * v, axis=1, keepdims=True) if t >= at else None
                for t in range(RANK // 8)
            ]
            scale = 1.0 / jnp.broadcast_to(dots[at][sub : sub + 1, :], (8, 1))
            for t in range(at, RANK // 8):
                coef = dots[t] * scale
                if t == at:
                    coef = jnp.where(row > sub, coef, 0.0)
                tiles[t] = tiles[t] - coef * v
    return [
        jnp.concatenate(
            [t * lax.rsqrt(jnp.sum(t * t, axis=1, keepdims=True)) for t in tiles], axis=0
        )
        for tiles in panel
    ]


class Compression:
    def __init__(self, first, refs, grads, error_in, q_init, update, error_out):
        self.first = first
        self.part16, self.got16, self.crop16, self.chunk, self.got32, self.mean, self.send, self.recv = refs
        self.grads, self.error_in, self.q_init = grads, error_in, q_init
        self.update, self.error_out = update, error_out
        self.me, self.dp = lax.axis_index("dap"), lax.axis_index("dp")
        self.mine = pl.ds(pl.multiple_of(self.me * PART, PART), PART)
        self.others = pl.ds(0, 2 * C - PART)
        self.replicas = pl.ds(0, DP - 1)

    def scatter(self):
        for w in range(2):
            self.part16[w * C : (w + 1) * C, :] = self.grads[self.first + w].astype(BF16)
        for t, peer in enumerate(peers()):
            block = self.part16.at[pl.ds(pl.multiple_of(peer * PART, PART), PART)]
            remote(block, self.got16.at[t], self.send.at[0], self.recv.at[0], "dap", peer)

    def across(self):
        await_bytes(self.got16, self.recv.at[0])
        total = self.part16[self.mine, :].astype(F32)
        for t in range(DAP - 1):
            total = total + self.got16[t].astype(F32)
        self.crop16[self.mine, :] = (total * (1.0 / N)).astype(BF16)
        matrix = self.first + self.me // 8
        row = pl.multiple_of(lax.rem(self.me, 8) * PART, PART)
        self.chunk[...] = self.crop16[self.mine, :].astype(F32) + self.error_in[matrix, pl.ds(row, PART), :]
        self.got32[self.dp] = self.chunk[...]
        for s in range(1, DP):
            peer = lax.rem(self.dp + s, DP)
            remote(self.chunk, self.got32.at[self.dp], self.send.at[1], self.recv.at[1], "dp", peer)

    def share(self):
        for peer in peers():
            block = self.crop16.at[self.mine]
            remote(block, block, self.send.at[2], self.recv.at[2], "dap", peer)

    def gather(self):
        await_bytes(self.got32.at[self.replicas], self.recv.at[1])
        total = self.got32[0]
        for r in range(1, DP):
            total = total + self.got32[r]
        self.mean[self.mine, :] = total * (1.0 / DP)
        for peer in peers():
            block = self.mean.at[self.mine]
            remote(block, block, self.send.at[3], self.recv.at[3], "dap", peer)

    def finish(self):
        await_bytes(self.mean.at[self.others], self.recv.at[3])
        panel = []
        for w in range(2):
            rows = exact(self.q_init[self.first + w], self.mean[w * C : (w + 1) * C, :], 1, 1)
            panel.append([rows[t * 8 : (t + 1) * 8, :] for t in range(RANK // 8)])
        basis = gram_schmidt(panel)
        await_bytes(self.crop16.at[self.others], self.recv.at[2])
        for w in range(2):
            here = slice(w * C, (w + 1) * C)
            coeffs = exact(basis[w], self.mean[here, :], 1, 0)
            new = exact(basis[w], coeffs, 0, 0)
            self.update[self.first + w] = new
            memory = self.crop16[here, :].astype(F32) + self.error_in[self.first + w]
            self.error_out[self.first + w] = memory - new

    def sent(self):
        await_bytes(self.part16.at[self.others], self.send.at[0])
        await_bytes(self.got32.at[self.replicas], self.send.at[1])
        await_bytes(self.crop16.at[self.others], self.send.at[2])
        await_bytes(self.mean.at[self.others], self.send.at[3])


def main_kernel(
    pair_in, cot_in, error_at, q_at, residue, weights, out, update, error_out,
    pair, cot, error_in, q_init,
    grads, mask, lr_t, lr, gate_t, normed, normed_t, gate, grad_proj, z_hat, z_inv, from_gate,
    h_mean, x_mean, x_inv, tall, both,
    send_l, send_r, left, right, prod, x, send_g, grad, to_l, to_r, got_l, got_r,
    fetch, send, recv, *shared,
):
    size = len(shared) // 2
    late = Compression(0, shared[:size], grads, error_in, q_init, update, error_out)
    early = Compression(2, shared[size:], grads, error_in, q_init, update, error_out)
    fetched = []
    for k, (src, dst) in enumerate(
        [
            (pair_in.at[:, pl.ds(0, 128)], pair.at[:, pl.ds(0, 128)]),
            (pair_in.at[:, pl.ds(128, 128)], pair.at[:, pl.ds(128, 128)]),
            (cot_in, cot),
            (error_at, error_in),
            (q_at, q_init),
        ]
    ):
        copy = pltpu.make_async_copy(src, dst, fetch.at[k])
        copy.start()
        fetched.append(copy)
    greet()
    set_up(residue, weights, mask, lr_t, lr, gate_t)
    started = []

    def begin(k, half, group, src, dst):
        exchange(src, dst, half, group, send.at[k], recv.at[k])
        if group == 0:
            started.append((src, half, k))

    def arrive(k, half, group, dst):
        await_bytes(dst.at[half, :, pl.ds(group * GROUP, GROUP)], recv.at[k, half, group])

    sides = [(send_l, left), (send_r, right)]
    for half in range(2):
        fetched[half].wait()
        front(half, pair, lr_t, normed, normed_t, z_hat, z_inv, tall)
        for w, (src, dst) in enumerate(sides):
            pack(tall, w, half, mask, src)
            if half == 0 and w == 0:
                greeted()
            begin(w, half, 0, src, dst)
    for half in range(2):
        for w, (src, dst) in enumerate(sides):
            begin(w, half, 1, src, dst)
    for copy in fetched[2:]:
        copy.wait()
    for half in range(2):
        gating(half, cot, normed, weights, gate, grad_proj, tall, h_mean)
    for group in range(2):
        for half in range(2):
            for w in range(2):
                arrive(w, half, group, sides[w][1])
        first_triangle(0, group, left, right, prod)
        begin(2, 0, group, prod, x)
    for group in range(2):
        first_triangle(1, group, left, right, prod)
        begin(2, 1, group, prod, x)
    for half in range(2):
        for group in range(2):
            arrive(2, half, group, x)
        mid_core(half, x, tall, h_mean, x_mean, x_inv, send_g)
        for group in range(2):
            begin(3, half, group, send_g, grad)
        mid_rest(
            half, x, x_mean, x_inv, cot, normed_t, gate, grad_proj, weights, gate_t,
            tall, from_gate, grads,
        )
    early.scatter()
    for group in range(2):
        for half in range(2):
            arrive(3, half, group, grad)
        grad_of_left(0, group, grad, right, to_l)
        begin(4, 0, group, to_l, got_l)
        grad_of_right(0, group, grad, left, to_r)
        begin(5, 0, group, to_r, got_r)
    for k in range(2):
        for group in range(2):
            if k == 0:
                grad_of_left(1, group, grad, right, to_l)
                begin(4, 1, group, to_l, got_l)
            else:
                grad_of_right(1, group, grad, left, to_r)
                begin(5, 1, group, to_r, got_r)
    early.across()
    for half in range(2):
        for w, src in enumerate([got_l, got_r]):
            for group in range(2):
                arrive(4 + w, half, group, src)
            unpack(src, w, half, mask, tall)
            last_grads(half, w, tall, normed, both, grads)
        if half == 0:
            last_pair(half, both, z_hat, z_inv, from_gate, lr, out)
    late.scatter()
    early.gather()
    early.share()
    last_pair(1, both, z_hat, z_inv, from_gate, lr, out)
    late.across()
    late.gather()
    late.share()
    early.finish()
    late.finish()
    late.sent()
    early.sent()
    for src, half, k in started:
        await_bytes(src.at[half, pl.ds(0, DAP - 1)], send.at[k, half])


def main_call(*operands):
    vmem = pl.BlockSpec(memory_space=pltpu.VMEM)
    hbm = pl.BlockSpec(memory_space=pl.ANY)
    blocks = pltpu.VMEM((2, DAP, SLICE, ROWS, 128), BF16)
    wide = pltpu.VMEM((ROWS, N, C), F32)
    half_wide = pltpu.VMEM((ROWS, N, C), BF16)
    return pl.pallas_call(
        main_kernel,
        name="triangle",
        out_shape=(
            pltpu.VMEM((ROWS, N, C), BF16),
            pltpu.VMEM((4, C, C), F32),
            pltpu.VMEM((4, C, C), F32),
        ),
        in_specs=[hbm] * 4 + [vmem] * 2,
        out_specs=(vmem, vmem, vmem),
        scratch_shapes=[
            half_wide,
            half_wide,
            pltpu.VMEM((4, C, C), F32),
            pltpu.VMEM((4, RANK, C), F32),
            pltpu.VMEM((4, C, C), F32),
            pltpu.VMEM((ROWS, N), F32),
            pltpu.VMEM((2 * C, C), BF16),
            pltpu.VMEM((C, 2 * C), BF16),
            pltpu.VMEM((C, C), BF16),
            half_wide,
            pltpu.VMEM((2, ROWS, C, 128), BF16),
            wide,
            half_wide,
            wide,
            wide,
            wide,
            pltpu.VMEM((ROWS, N), F32),
            pltpu.VMEM((ROWS, N), F32),
            pltpu.VMEM((ROWS, N), F32),
            pltpu.VMEM((2, 2, C * PITCH, 128), F32),
            pltpu.VMEM((ROWS, 2 * C, 128), BF16),
        ]
        + [blocks] * 12
        + [
            pltpu.SemaphoreType.DMA((5,)),
            pltpu.SemaphoreType.DMA((6, 2)),
            pltpu.SemaphoreType.DMA((6, 2, 2)),
        ]
        + [
            pltpu.VMEM((2 * C, C), BF16),
            pltpu.VMEM((DAP - 1, PART, C), BF16),
            pltpu.VMEM((2 * C, C), BF16),
            pltpu.VMEM((PART, C), F32),
            pltpu.VMEM((DP, PART, C), F32),
            pltpu.VMEM((2 * C, C), F32),
            pltpu.SemaphoreType.DMA((4,)),
            pltpu.SemaphoreType.DMA((4,)),
        ]
        * 2,
        compiler_params=pltpu.CompilerParams(
            collective_id=0, has_side_effects=True, vmem_limit_bytes=56 << 20
        ),
    )(*operands)


def store_kernel(*refs):
    sources, targets, sems = refs[:3], refs[3:6], refs[6]
    copies = [
        pltpu.make_async_copy(src, dst, sems.at[k])
        for k, (src, dst) in enumerate(zip(sources, targets))
    ]
    for copy in copies:
        copy.start()
    for copy in copies:
        copy.wait()


def store(*arrays):
    vmem = pl.BlockSpec(memory_space=pltpu.VMEM)
    hbm = pl.BlockSpec(memory_space=pl.ANY)
    return pl.pallas_call(
        store_kernel,
        name="store",
        out_shape=tuple(jax.ShapeDtypeStruct(a.shape, a.dtype) for a in arrays),
        in_specs=[vmem] * 3,
        out_specs=(hbm,) * 3,
        scratch_shapes=[pltpu.SemaphoreType.DMA((3,))],
        compiler_params=pltpu.CompilerParams(vmem_limit_bytes=8 << 20),
    )(*arrays)


def per_device(pair_act, cotangent, residue_mask, weights, error_in, q_init):
    results = main_call(
        pair_act[0], cotangent[0], error_in[0], q_init.transpose(0, 2, 1), residue_mask, weights
    )
    grad_pair, update, error_out = store(*results)
    return (grad_pair[None], update, error_out[None])


def solution(mesh):
    placed = (
        P("dp", "dap", None, None),
        P("dp", "dap", None, None),
        P("dp", None),
        P(),
        P("dp", None, None, None),
        P(),
    )
    return jax.shard_map(
        per_device,
        mesh=mesh,
        in_specs=placed,
        out_specs=(P("dp", "dap", None, None), P(), P("dp", None, None, None)),
        check_vma=False,
    )
```

```python
import functools

import jax
import jax.numpy as jnp
from jax import lax
from jax.experimental import pallas as pl
from jax.experimental.pallas import tpu as pltpu
from jax.sharding import PartitionSpec as P

EPS = 1e-05
HIGH = lax.Precision.HIGHEST
MESH = pl.DeviceIdType.MESH
F32 = jnp.float32
BF16 = jnp.bfloat16
C = 128
N = 256
ROWS = 16
SLICE = 8
GROUP = 4
AHEAD = 3
PITCH = 17
RANK = 32
DAP = 16
DP = 8
PART = 2 * C // DAP
OFFSETS = [(2,2),(1,2),(3,2),(2,1),(2,3),(1,1),(3,3),(1,3),(3,1),(2,0),(0,2),(1,0),(3,0),(0,1),(0,3)]


def nn(a, b):
    return lax.dot_general(a, b, (((1,), (0,)), ((), ())), preferred_element_type=F32)


def nt(a, b):
    return lax.dot_general(a, b, (((1,), (1,)), ((), ())), preferred_element_type=F32)


def exact(a, b, a_dim, b_dim):
    dims = (((a_dim,), (b_dim,)), ((), ()))
    return lax.dot_general(a, b, dims, preferred_element_type=F32, precision=HIGH)


def tn(a, b):
    return lax.dot_general(a, b, (((0,), (0,)), ((), ())), preferred_element_type=F32)


def peers():
    me = lax.axis_index("dap")
    y, z = me // 4, lax.rem(me, 4)
    sign = 1 - 2 * lax.rem(lax.axis_index("dp"), 2)
    return [
        lax.rem(y + sign * dy + 4, 4) * 4 + lax.rem(z + sign * dz + 4, 4)
        for dy, dz in OFFSETS
    ]


def greet():
    barrier = pltpu.get_barrier_semaphore()
    for axis, size in (("dap", DAP), ("dp", DP)):
        me = lax.axis_index(axis)
        for step in range(1, size):
            pl.semaphore_signal(
                barrier, inc=1, device_id={axis: lax.rem(me + step, size)}, device_id_type=MESH
            )


def greeted():
    pl.semaphore_wait(pltpu.get_barrier_semaphore(), DAP + DP - 2)


def remote(src, dst, send, recv, axis, peer):
    copy = pltpu.make_async_remote_copy(
        src_ref=src, dst_ref=dst, send_sem=send, recv_sem=recv,
        device_id={axis: peer}, device_id_type=MESH,
    )
    copy.start()
    return copy


def exchange(src, dst, half, group, send, recv):
    me = lax.axis_index("dap")
    these = pl.ds(0, SLICE) if group is None else pl.ds(group * GROUP, GROUP)
    arrived = recv.at[half, group or 0]
    for peer in peers():
        remote(
            src.at[half, peer, these], dst.at[half, me, these], send.at[half], arrived, "dap", peer
        )
    pltpu.make_async_copy(src.at[half, me, these], dst.at[half, me, these], arrived).start()


def await_bytes(ref, sem):
    pltpu.make_async_copy(ref, ref, sem).wait()


def set_up(residue, weights, mask, lr_t, lr, gate_t):
    me = lax.axis_index("dap")
    keep = residue[...].astype(F32)
    col = lax.broadcasted_iota(jnp.int32, (ROWS, N), 1)
    row = lax.broadcasted_iota(jnp.int32, (ROWS, N), 0) + me * ROWS
    keep_rows = jnp.sum(jnp.where(col == row, keep, 0.0), axis=1, keepdims=True)
    mask[...] = keep_rows * keep
    for w in range(2):
        lr_t[w * C : (w + 1) * C, :] = weights[w].astype(F32).T.astype(BF16)
        lr[:, w * C : (w + 1) * C] = weights[w]
    gate_t[...] = weights[2].astype(F32).T.astype(BF16)


def front(half, pair, lr_t, normed, normed_t, z_hat, z_inv, tall):
    lanes = slice(half * 128, (half + 1) * 128)

    def step(p, _):
        turned = []
        for i in (2 * p, 2 * p + 1):
            x = pair[i, lanes, :].astype(F32)
            centre = x - jnp.sum(x, axis=-1, keepdims=True) * (1.0 / C)
            inv = lax.rsqrt(jnp.sum(centre * centre, axis=-1, keepdims=True) * (1.0 / C) + EPS)
            z = centre * inv
            nb = z.astype(BF16)
            turned.append(nb.T)
            normed[i, lanes, :] = nb
            normed_t[half, i] = turned[-1]
            z_hat[i, lanes, :] = z
            z_inv[i, lanes, :] = jnp.broadcast_to(inv, (128, C))
        both = nn(lr_t[...], jnp.concatenate(turned, axis=1))
        for u in range(2):
            for w in range(2):
                tall.at[w, half][pl.ds(2 * p + u, C, stride=PITCH), :] = both[
                    w * C : (w + 1) * C, u * 128 : (u + 1) * 128
                ]
        return 0

    lax.fori_loop(0, ROWS // 2, step, 0, unroll=4)


def gating(half, cot, normed, weights, gate, grad_proj, tall, h_mean):
    lanes = slice(half * 128, (half + 1) * 128)

    def step(i, _):
        g = jax.nn.sigmoid(nn(normed[i, lanes, :], weights[2]))
        gp = (cot[i, lanes, :].astype(F32) * g).astype(BF16)
        gate[i, lanes, :] = g
        grad_proj[i, lanes, :] = gp
        tall.at[1, half][pl.ds(i, C, stride=PITCH), :] = nt(weights[3], gp)
        return 0

    lax.fori_loop(0, ROWS, step, 0, unroll=4)

    def total(b, acc):
        for u in range(SLICE):
            acc = acc + tall[1, half, tile_at(b, u), :]
        return acc

    zero = jnp.zeros((ROWS, 128), F32)
    h_mean[:, lanes] = lax.fori_loop(0, DAP, total, zero) * (1.0 / C)


def tile_at(b, u):
    return pl.ds(b * SLICE * PITCH + u * PITCH, ROWS)


def pack(tall, w, half, mask, dst):
    m = mask[:, half * 128 : (half + 1) * 128]

    def step(b, _):
        for u in range(SLICE):
            dst[half, b, u] = (tall[w, half, tile_at(b, u), :] * m).astype(BF16)
        return 0

    lax.fori_loop(0, DAP, step, 0)


def plane(ref, half, c):
    return ref[half, :, c].reshape(N, 128)


def whole(ref, c):
    return jnp.concatenate([plane(ref, 0, c), plane(ref, 1, c)], axis=1)


def first_triangle(half, group, left, right, prod):
    def step(c, _):
        cols = right[:, half * DAP // 2 : (half + 1) * DAP // 2, c]
        cols = jnp.concatenate([cols[0].reshape(128, 128), cols[1].reshape(128, 128)], axis=1)
        prod[half, :, c] = nt(whole(left, c), cols).astype(BF16).reshape(DAP, ROWS, 128)
        return 0

    lax.fori_loop(group * GROUP, (group + 1) * GROUP, step, 0, unroll=4)


def mid_core(half, x, tall, h_mean, x_mean, x_inv, dst):
    lanes = slice(half * 128, (half + 1) * 128)
    zero = jnp.zeros((ROWS, 128), F32)

    def total(b, acc):
        for u in range(SLICE):
            acc = acc + x[half, b, u].astype(F32)
        return acc

    mean = lax.fori_loop(0, DAP, total, zero) * (1.0 / C)

    def square(b, acc):
        squares, dots = acc
        for u in range(SLICE):
            d = x[half, b, u].astype(F32) - mean
            squares = squares + d * d
            dots = dots + d * tall[1, half, tile_at(b, u), :]
        return squares, dots

    squares, dots = lax.fori_loop(0, DAP, square, (zero, zero))
    inv = lax.rsqrt(squares * (1.0 / C) + EPS)
    second = dots * inv * (1.0 / C)
    first = h_mean[:, lanes]
    x_mean[:, lanes] = mean
    x_inv[:, lanes] = inv

    def store(b, _):
        for u in range(SLICE):
            x_hat = (x[half, b, u].astype(F32) - mean) * inv
            v = inv * (tall[1, half, tile_at(b, u), :] - first - x_hat * second)
            dst[half, b, u] = v.astype(BF16)
        return 0

    lax.fori_loop(0, DAP, store, 0)


def mid_rest(half, x, x_mean, x_inv, cot, normed_t, gate, grad_proj, weights, gate_t, tall, from_gate, grads):
    lanes = slice(half * 128, (half + 1) * 128)
    mean = x_mean[:, lanes]
    inv = x_inv[:, lanes]

    def store(b, _):
        for u in range(SLICE):
            tall[0, half, tile_at(b, u), :] = (x[half, b, u].astype(F32) - mean) * inv
        return 0

    lax.fori_loop(0, DAP, store, 0)

    def step(i, carry):
        gate_grad, out_grad = carry
        xn = tall.at[0, half][pl.ds(i, C, stride=PITCH), :].astype(BF16)
        projected = tn(xn, weights[3])
        g = gate[i, lanes, :]
        up = cot[i, lanes, :].astype(F32)
        grad_logit = (up * projected * g * (1.0 - g)).astype(BF16)
        from_gate[i, lanes, :] = nn(grad_logit, gate_t[...])
        gate_grad = gate_grad + nn(normed_t[half, i], grad_logit)
        out_grad = out_grad + nn(xn, grad_proj[i, lanes, :])
        return gate_grad, out_grad

    zero = jnp.zeros((C, C), F32)
    new = lax.fori_loop(0, ROWS, step, (zero, zero), unroll=4)
    for w in range(2):
        grads[2 + w] = new[w] if half == 0 else grads[2 + w] + new[w]


def grad_of_left(half, group, grad, right, dst):
    def step(c, _):
        dst[half, :, c] = nn(whole(grad, c), plane(right, half, c)).astype(BF16).reshape(DAP, ROWS, 128)
        return 0

    lax.fori_loop(group * GROUP, (group + 1) * GROUP, step, 0, unroll=4)


def grad_of_right(half, group, grad, left, dst):
    def step(c, _):
        dst[half, :, c] = tn(whole(grad, c), plane(left, half, c)).astype(BF16).reshape(DAP, ROWS, 128)
        return 0

    lax.fori_loop(group * GROUP, (group + 1) * GROUP, step, 0, unroll=4)


def unpack(src, w, half, mask, tall):
    m = mask[:, half * 128 : (half + 1) * 128]

    def step(b, _):
        for u in range(SLICE):
            tall[w, half, tile_at(b, u), :] = src[half, b, u].astype(F32) * m
        return 0

    lax.fori_loop(0, DAP, step, 0)


def last_grads(half, w, tall, normed, both, grads):
    lanes = slice(half * 128, (half + 1) * 128)
    rows = slice(w * C, (w + 1) * C)

    def step(p, acc):
        sides = []
        for i in (2 * p, 2 * p + 1):
            sides.append(tall.at[w, half][pl.ds(i, C, stride=PITCH), :].astype(BF16))
            both[i, rows, :] = sides[-1]
        cells = jnp.concatenate([normed[2 * p, lanes, :], normed[2 * p + 1, lanes, :]], axis=0)
        return acc + nn(jnp.concatenate(sides, axis=1), cells)

    acc = lax.fori_loop(0, ROWS // 2, step, jnp.zeros((C, C), F32), unroll=4).T
    grads[w] = acc if half == 0 else grads[w] + acc


def last_pair(half, both, z_hat, z_inv, from_gate, lr, out):
    lanes = slice(half * 128, (half + 1) * 128)

    def step(i, _):
        grad = nn(lr[...], both[i]).T + from_gate[i, lanes, :]
        z = z_hat[i, lanes, :]
        first = jnp.sum(grad, axis=-1, keepdims=True) * (1.0 / C)
        second = jnp.sum(grad * z, axis=-1, keepdims=True) * (1.0 / C)
        out[i, lanes, :] = (z_inv[i, lanes, :] * (grad - first - z * second)).astype(BF16)
        return 0

    lax.fori_loop(0, ROWS, step, 0, unroll=4)


def gram_schmidt(panel):
    lane = lax.broadcasted_iota(jnp.int32, (1, C), 1)
    within = lax.rem(lane, RANK)

    def spread(j):
        return jnp.where(
            lane < RANK,
            jnp.broadcast_to(panel[:, j : j + 1], (C, C)),
            jnp.broadcast_to(panel[:, RANK + j : RANK + j + 1], (C, C)),
        )

    coming = {j: spread(j) for j in range(AHEAD + 1)}
    for j in range(RANK):
        v = coming.pop(j)
        per = 1.0 / jnp.sum(v * v, axis=0, keepdims=True)
        for k in list(coming):
            alpha = jnp.sum(coming[k] * v, axis=0, keepdims=True) * per
            coming[k] = coming[k] - alpha * v
        on_v = jnp.sum(panel * v, axis=0, keepdims=True) * per
        panel = panel - jnp.where(within > j, on_v, 0.0) * v
        if j + AHEAD + 1 < RANK:
            coming[j + AHEAD + 1] = spread(j + AHEAD + 1)
    unit = panel * lax.rsqrt(jnp.sum(panel * panel, axis=0, keepdims=True))
    return jnp.where(lane < 2 * RANK, unit, 0.0)


class Compression:
    def __init__(self, first, refs, grads, error_in, q_init, update, error_out):
        self.first = first
        self.part16, self.got16, self.crop16, self.chunk, self.got32, self.mean, self.send, self.recv = refs
        self.grads, self.error_in, self.q_init = grads, error_in, q_init
        self.update, self.error_out = update, error_out
        self.me, self.dp = lax.axis_index("dap"), lax.axis_index("dp")
        self.mine = pl.ds(pl.multiple_of(self.me * PART, PART), PART)
        self.others = pl.ds(0, 2 * C - PART)
        self.replicas = pl.ds(0, DP - 1)

    def scatter(self):
        for w in range(2):
            self.part16[w * C : (w + 1) * C, :] = self.grads[self.first + w].astype(BF16)
        for t, peer in enumerate(peers()):
            block = self.part16.at[pl.ds(pl.multiple_of(peer * PART, PART), PART)]
            remote(block, self.got16.at[t], self.send.at[0], self.recv.at[0], "dap", peer)

    def across(self):
        await_bytes(self.got16, self.recv.at[0])
        total = self.part16[self.mine, :].astype(F32)
        for t in range(DAP - 1):
            total = total + self.got16[t].astype(F32)
        self.crop16[self.mine, :] = (total * (1.0 / N)).astype(BF16)
        matrix = self.first + self.me // 8
        row = pl.multiple_of(lax.rem(self.me, 8) * PART, PART)
        self.chunk[...] = self.crop16[self.mine, :].astype(F32) + self.error_in[matrix, pl.ds(row, PART), :]
        self.got32[self.dp] = self.chunk[...]
        for s in range(1, DP):
            peer = lax.rem(self.dp + s, DP)
            remote(self.chunk, self.got32.at[self.dp], self.send.at[1], self.recv.at[1], "dp", peer)

    def share(self):
        for peer in peers():
            block = self.crop16.at[self.mine]
            remote(block, block, self.send.at[2], self.recv.at[2], "dap", peer)

    def gather(self):
        await_bytes(self.got32.at[self.replicas], self.recv.at[1])
        total = self.got32[0]
        for r in range(1, DP):
            total = total + self.got32[r]
        self.mean[self.mine, :] = total * (1.0 / DP)
        for peer in peers():
            block = self.mean.at[self.mine]
            remote(block, block, self.send.at[3], self.recv.at[3], "dap", peer)

    def finish(self):
        await_bytes(self.mean.at[self.others], self.recv.at[3])
        panel = sum(
            exact(self.mean[w * C : (w + 1) * C, :], self.q_init[self.first + w], 1, 0) for w in range(2)
        )
        basis = gram_schmidt(panel)
        rows = basis.T
        lane = lax.broadcasted_iota(jnp.int32, (1, C), 1)
        await_bytes(self.crop16.at[self.others], self.recv.at[2])
        for w in range(2):
            here = slice(w * C, (w + 1) * C)
            coeffs = exact(rows, self.mean[here, :], 1, 0)
            new = exact(jnp.where(lane // RANK == w, basis, 0.0), coeffs, 1, 0)
            self.update[self.first + w] = new
            memory = self.crop16[here, :].astype(F32) + self.error_in[self.first + w]
            self.error_out[self.first + w] = memory - new

    def sent(self):
        await_bytes(self.part16.at[self.others], self.send.at[0])
        await_bytes(self.got32.at[self.replicas], self.send.at[1])
        await_bytes(self.crop16.at[self.others], self.send.at[2])
        await_bytes(self.mean.at[self.others], self.send.at[3])


def main_kernel(
    pair_in, cot_in, error_at, q_at, residue, weights, out, update, error_out,
    pair, cot, error_in, q_init, q_wide,
    grads, mask, lr_t, lr, gate_t, normed, normed_t, gate, grad_proj, z_hat, z_inv, from_gate,
    h_mean, x_mean, x_inv, tall, both,
    send_l, send_r, left, right, prod, x, send_g, grad, to_l, to_r, got_l, got_r,
    fetch, send, recv, *shared,
):
    size = len(shared) // 2
    late = Compression(0, shared[:size], grads, error_in, q_wide, update, error_out)
    early = Compression(2, shared[size:], grads, error_in, q_wide, update, error_out)
    fetched = []
    for k, (src, dst) in enumerate(
        [
            (pair_in.at[:, pl.ds(0, 128)], pair.at[:, pl.ds(0, 128)]),
            (pair_in.at[:, pl.ds(128, 128)], pair.at[:, pl.ds(128, 128)]),
            (cot_in, cot),
            (error_at, error_in),
            (q_at, q_init),
        ]
    ):
        copy = pltpu.make_async_copy(src, dst, fetch.at[k])
        copy.start()
        fetched.append(copy)
    greet()
    set_up(residue, weights, mask, lr_t, lr, gate_t)
    started = []

    def begin(k, half, group, src, dst):
        exchange(src, dst, half, group, send.at[k], recv.at[k])
        if not group:
            started.append((src, half, k))

    def arrive(k, half, group, dst):
        these = pl.ds(0, SLICE) if group is None else pl.ds(group * GROUP, GROUP)
        await_bytes(dst.at[half, :, these], recv.at[k, half, group or 0])

    sides = [(send_l, left), (send_r, right)]
    for half in range(2):
        fetched[half].wait()
        front(half, pair, lr_t, normed, normed_t, z_hat, z_inv, tall)
        for w, (src, dst) in enumerate(sides):
            pack(tall, w, half, mask, src)
            if half == 0 and w == 0:
                greeted()
            begin(w, half, 0, src, dst)
    for half in range(2):
        for w, (src, dst) in enumerate(sides):
            begin(w, half, 1, src, dst)
    for copy in fetched[2:]:
        copy.wait()
    for w in range(4):
        parts = [q_init[w], jnp.zeros((C - RANK, C), F32)]
        if w % 2:
            parts = [jnp.zeros((RANK, C), F32), q_init[w], jnp.zeros((C - 2 * RANK, C), F32)]
        q_wide[w] = jnp.concatenate(parts, axis=0).T
    for half in range(2):
        gating(half, cot, normed, weights, gate, grad_proj, tall, h_mean)
    for group in range(2):
        for half in range(2):
            for w in range(2):
                arrive(w, half, group, sides[w][1])
        first_triangle(0, group, left, right, prod)
        begin(2, 0, group, prod, x)
    for group in range(2):
        first_triangle(1, group, left, right, prod)
    begin(2, 1, None, prod, x)
    for half in range(2):
        for group in range(2) if half == 0 else [None]:
            arrive(2, half, group, x)
        mid_core(half, x, tall, h_mean, x_mean, x_inv, send_g)
        for group in [None] if half == 0 else range(2):
            begin(3, half, group, send_g, grad)
        mid_rest(
            half, x, x_mean, x_inv, cot, normed_t, gate, grad_proj, weights, gate_t,
            tall, from_gate, grads,
        )
    early.scatter()
    for group in range(2):
        if group == 0:
            arrive(3, 0, None, grad)
        arrive(3, 1, group, grad)
        grad_of_left(0, group, grad, right, to_l)
        begin(4, 0, group, to_l, got_l)
        grad_of_right(0, group, grad, left, to_r)
        begin(5, 0, group, to_r, got_r)
    for group in range(2):
        grad_of_left(1, group, grad, right, to_l)
    begin(4, 1, None, to_l, got_l)
    for group in range(2):
        grad_of_right(1, group, grad, left, to_r)
    begin(5, 1, None, to_r, got_r)
    early.across()
    for half in range(2):
        for w, src in enumerate([got_l, got_r]):
            for group in range(2) if half == 0 else [None]:
                arrive(4 + w, half, group, src)
            unpack(src, w, half, mask, tall)
            last_grads(half, w, tall, normed, both, grads)
        if half == 0:
            last_pair(half, both, z_hat, z_inv, from_gate, lr, out)
    late.scatter()
    early.gather()
    early.share()
    last_pair(1, both, z_hat, z_inv, from_gate, lr, out)
    late.across()
    late.gather()
    late.share()
    early.finish()
    late.finish()
    late.sent()
    early.sent()
    for src, half, k in started:
        await_bytes(src.at[half, pl.ds(0, DAP - 1)], send.at[k, half])


def main_call(*operands):
    vmem = pl.BlockSpec(memory_space=pltpu.VMEM)
    hbm = pl.BlockSpec(memory_space=pl.ANY)
    blocks = pltpu.VMEM((2, DAP, SLICE, ROWS, 128), BF16)
    wide = pltpu.VMEM((ROWS, N, C), F32)
    half_wide = pltpu.VMEM((ROWS, N, C), BF16)
    return pl.pallas_call(
        main_kernel,
        name="triangle",
        out_shape=(
            pltpu.VMEM((ROWS, N, C), BF16),
            pltpu.VMEM((4, C, C), F32),
            pltpu.VMEM((4, C, C), F32),
        ),
        in_specs=[hbm] * 4 + [vmem] * 2,
        out_specs=(vmem, vmem, vmem),
        scratch_shapes=[
            half_wide,
            half_wide,
            pltpu.VMEM((4, C, C), F32),
            pltpu.VMEM((4, RANK, C), F32),
            pltpu.VMEM((4, C, C), F32),
            pltpu.VMEM((4, C, C), F32),
            pltpu.VMEM((ROWS, N), F32),
            pltpu.VMEM((2 * C, C), BF16),
            pltpu.VMEM((C, 2 * C), BF16),
            pltpu.VMEM((C, C), BF16),
            half_wide,
            pltpu.VMEM((2, ROWS, C, 128), BF16),
            wide,
            half_wide,
            wide,
            wide,
            wide,
            pltpu.VMEM((ROWS, N), F32),
            pltpu.VMEM((ROWS, N), F32),
            pltpu.VMEM((ROWS, N), F32),
            pltpu.VMEM((2, 2, C * PITCH, 128), F32),
            pltpu.VMEM((ROWS, 2 * C, 128), BF16),
        ]
        + [blocks] * 12
        + [
            pltpu.SemaphoreType.DMA((5,)),
            pltpu.SemaphoreType.DMA((6, 2)),
            pltpu.SemaphoreType.DMA((6, 2, 2)),
        ]
        + [
            pltpu.VMEM((2 * C, C), BF16),
            pltpu.VMEM((DAP - 1, PART, C), BF16),
            pltpu.VMEM((2 * C, C), BF16),
            pltpu.VMEM((PART, C), F32),
            pltpu.VMEM((DP, PART, C), F32),
            pltpu.VMEM((2 * C, C), F32),
            pltpu.SemaphoreType.DMA((4,)),
            pltpu.SemaphoreType.DMA((4,)),
        ]
        * 2,
        compiler_params=pltpu.CompilerParams(
            collective_id=0, has_side_effects=True, vmem_limit_bytes=56 << 20
        ),
    )(*operands)


def store_kernel(*refs):
    sources, targets, sems = refs[:3], refs[3:6], refs[6]
    copies = [
        pltpu.make_async_copy(src, dst, sems.at[k])
        for k, (src, dst) in enumerate(zip(sources, targets))
    ]
    for copy in copies:
        copy.start()
    for copy in copies:
        copy.wait()


def store(*arrays):
    vmem = pl.BlockSpec(memory_space=pltpu.VMEM)
    hbm = pl.BlockSpec(memory_space=pl.ANY)
    return pl.pallas_call(
        store_kernel,
        name="store",
        out_shape=tuple(jax.ShapeDtypeStruct(a.shape, a.dtype) for a in arrays),
        in_specs=[vmem] * 3,
        out_specs=(hbm,) * 3,
        scratch_shapes=[pltpu.SemaphoreType.DMA((3,))],
        compiler_params=pltpu.CompilerParams(vmem_limit_bytes=8 << 20),
    )(*arrays)


def per_device(pair_act, cotangent, residue_mask, weights, error_in, q_init):
    results = main_call(
        pair_act[0], cotangent[0], error_in[0], q_init.transpose(0, 2, 1), residue_mask, weights
    )
    grad_pair, update, error_out = store(*results)
    return (grad_pair[None], update, error_out[None])


def solution(mesh):
    placed = (
        P("dp", "dap", None, None),
        P("dp", "dap", None, None),
        P("dp", None),
        P(),
        P("dp", None, None, None),
        P(),
    )
    return jax.shard_map(
        per_device,
        mesh=mesh,
        in_specs=placed,
        out_specs=(P("dp", "dap", None, None), P(), P("dp", None, None, None)),
        check_vma=False,
    )
```

```python
import functools

import jax
import jax.numpy as jnp
from jax import lax
from jax.experimental import pallas as pl
from jax.experimental.pallas import tpu as pltpu
from jax.sharding import PartitionSpec as P

EPS = 1e-05
HIGH = lax.Precision.HIGHEST
MESH = pl.DeviceIdType.MESH
F32 = jnp.float32
BF16 = jnp.bfloat16
C = 128
N = 256
ROWS = 16
SLICE = 8
GROUP = 4
AHEAD = 3
PITCH = 17
RANK = 32
DAP = 16
DP = 8
PART = 2 * C // DAP
OFFSETS = [(2,2),(1,2),(3,2),(2,1),(2,3),(1,1),(3,3),(1,3),(3,1),(2,0),(0,2),(1,0),(3,0),(0,1),(0,3)]


def nn(a, b):
    return lax.dot_general(a, b, (((1,), (0,)), ((), ())), preferred_element_type=F32)


def nt(a, b):
    return lax.dot_general(a, b, (((1,), (1,)), ((), ())), preferred_element_type=F32)


def exact(a, b, a_dim, b_dim):
    dims = (((a_dim,), (b_dim,)), ((), ()))
    return lax.dot_general(a, b, dims, preferred_element_type=F32, precision=HIGH)


def tn(a, b):
    return lax.dot_general(a, b, (((0,), (0,)), ((), ())), preferred_element_type=F32)


def peers():
    me = lax.axis_index("dap")
    y, z = me // 4, lax.rem(me, 4)
    sign = 1 - 2 * lax.rem(lax.axis_index("dp"), 2)
    return [
        lax.rem(y + sign * dy + 4, 4) * 4 + lax.rem(z + sign * dz + 4, 4)
        for dy, dz in OFFSETS
    ]


def greet():
    barrier = pltpu.get_barrier_semaphore()
    for axis, size in (("dap", DAP), ("dp", DP)):
        me = lax.axis_index(axis)
        for step in range(1, size):
            pl.semaphore_signal(
                barrier, inc=1, device_id={axis: lax.rem(me + step, size)}, device_id_type=MESH
            )


def greeted():
    pl.semaphore_wait(pltpu.get_barrier_semaphore(), DAP + DP - 2)


def remote(src, dst, send, recv, axis, peer):
    copy = pltpu.make_async_remote_copy(
        src_ref=src, dst_ref=dst, send_sem=send, recv_sem=recv,
        device_id={axis: peer}, device_id_type=MESH,
    )
    copy.start()
    return copy


def exchange(src, dst, half, group, send, recv):
    me = lax.axis_index("dap")
    these = pl.ds(0, SLICE) if group is None else pl.ds(group * GROUP, GROUP)
    arrived = recv.at[half, group or 0]
    for peer in peers():
        remote(
            src.at[half, peer, these], dst.at[half, me, these], send.at[half], arrived, "dap", peer
        )
    pltpu.make_async_copy(src.at[half, me, these], dst.at[half, me, these], arrived).start()


def await_bytes(ref, sem):
    pltpu.make_async_copy(ref, ref, sem).wait()


def set_up(residue, weights, mask, lr_t, lr, gate_t):
    me = lax.axis_index("dap")
    keep = residue[...].astype(F32)
    col = lax.broadcasted_iota(jnp.int32, (ROWS, N), 1)
    row = lax.broadcasted_iota(jnp.int32, (ROWS, N), 0) + me * ROWS
    keep_rows = jnp.sum(jnp.where(col == row, keep, 0.0), axis=1, keepdims=True)
    mask[...] = keep_rows * keep
    for w in range(2):
        lr_t[w * C : (w + 1) * C, :] = weights[w].astype(F32).T.astype(BF16)
        lr[:, w * C : (w + 1) * C] = weights[w]
    gate_t[...] = weights[2].astype(F32).T.astype(BF16)


def front(half, pair, lr_t, normed, normed_t, z_hat, z_inv, tall):
    lanes = slice(half * 128, (half + 1) * 128)

    def step(p, _):
        turned = []
        for i in (2 * p, 2 * p + 1):
            x = pair[i, lanes, :].astype(F32)
            centre = x - jnp.sum(x, axis=-1, keepdims=True) * (1.0 / C)
            inv = lax.rsqrt(jnp.sum(centre * centre, axis=-1, keepdims=True) * (1.0 / C) + EPS)
            z = centre * inv
            nb = z.astype(BF16)
            turned.append(nb.T)
            normed[i, lanes, :] = nb
            normed_t[half, i] = turned[-1]
            z_hat[i, lanes, :] = z
            z_inv[i, lanes, :] = jnp.broadcast_to(inv, (128, C))
        both = nn(lr_t[...], jnp.concatenate(turned, axis=1))
        for u in range(2):
            for w in range(2):
                tall.at[w, half][pl.ds(2 * p + u, C, stride=PITCH), :] = both[
                    w * C : (w + 1) * C, u * 128 : (u + 1) * 128
                ]
        return 0

    lax.fori_loop(0, ROWS // 2, step, 0, unroll=4)


def gating(half, cot, normed, weights, gate, grad_proj, tall, h_mean):
    lanes = slice(half * 128, (half + 1) * 128)

    def step(i, _):
        g = jax.nn.sigmoid(nn(normed[i, lanes, :], weights[2]))
        gp = (cot[i, lanes, :].astype(F32) * g).astype(BF16)
        gate[i, lanes, :] = g
        grad_proj[i, lanes, :] = gp
        tall.at[1, half][pl.ds(i, C, stride=PITCH), :] = nt(weights[3], gp)
        return 0

    lax.fori_loop(0, ROWS, step, 0, unroll=4)

    def total(b, acc):
        for u in range(SLICE):
            acc = acc + tall[1, half, tile_at(b, u), :]
        return acc

    zero = jnp.zeros((ROWS, 128), F32)
    h_mean[:, lanes] = lax.fori_loop(0, DAP, total, zero) * (1.0 / C)


def tile_at(b, u):
    return pl.ds(b * SLICE * PITCH + u * PITCH, ROWS)


def pack(tall, w, half, mask, dst):
    m = mask[:, half * 128 : (half + 1) * 128]

    def step(b, _):
        for u in range(SLICE):
            dst[half, b, u] = (tall[w, half, tile_at(b, u), :] * m).astype(BF16)
        return 0

    lax.fori_loop(0, DAP, step, 0)


def plane(ref, half, c):
    return ref[half, :, c].reshape(N, 128)


def whole(ref, c):
    return jnp.concatenate([plane(ref, 0, c), plane(ref, 1, c)], axis=1)


def first_triangle(half, group, left, right, prod):
    def step(c, _):
        cols = right[:, half * DAP // 2 : (half + 1) * DAP // 2, c]
        cols = jnp.concatenate([cols[0].reshape(128, 128), cols[1].reshape(128, 128)], axis=1)
        prod[half, :, c] = nt(whole(left, c), cols).astype(BF16).reshape(DAP, ROWS, 128)
        return 0

    lax.fori_loop(group * GROUP, (group + 1) * GROUP, step, 0, unroll=4)


def mid_core(half, x, tall, h_mean, x_mean, x_inv, dst):
    lanes = slice(half * 128, (half + 1) * 128)
    zero = jnp.zeros((ROWS, 128), F32)

    def total(b, acc):
        for u in range(SLICE):
            acc = acc + x[half, b, u].astype(F32)
        return acc

    mean = lax.fori_loop(0, DAP, total, zero) * (1.0 / C)

    def square(b, acc):
        squares, dots = acc
        for u in range(SLICE):
            d = x[half, b, u].astype(F32) - mean
            squares = squares + d * d
            dots = dots + d * tall[1, half, tile_at(b, u), :]
        return squares, dots

    squares, dots = lax.fori_loop(0, DAP, square, (zero, zero))
    inv = lax.rsqrt(squares * (1.0 / C) + EPS)
    second = dots * inv * (1.0 / C)
    first = h_mean[:, lanes]
    x_mean[:, lanes] = mean
    x_inv[:, lanes] = inv

    def store(b, _):
        for u in range(SLICE):
            x_hat = (x[half, b, u].astype(F32) - mean) * inv
            v = inv * (tall[1, half, tile_at(b, u), :] - first - x_hat * second)
            dst[half, b, u] = v.astype(BF16)
        return 0

    lax.fori_loop(0, DAP, store, 0)


def mid_rest(half, x, x_mean, x_inv, cot, normed_t, gate, grad_proj, weights, gate_t, tall, from_gate, grads):
    lanes = slice(half * 128, (half + 1) * 128)
    mean = x_mean[:, lanes]
    inv = x_inv[:, lanes]

    def store(b, _):
        for u in range(SLICE):
            tall[0, half, tile_at(b, u), :] = (x[half, b, u].astype(F32) - mean) * inv
        return 0

    lax.fori_loop(0, DAP, store, 0)

    def step(i, carry):
        gate_grad, out_grad = carry
        xn = tall.at[0, half][pl.ds(i, C, stride=PITCH), :].astype(BF16)
        projected = tn(xn, weights[3])
        g = gate[i, lanes, :]
        up = cot[i, lanes, :].astype(F32)
        grad_logit = (up * projected * g * (1.0 - g)).astype(BF16)
        from_gate[i, lanes, :] = nn(grad_logit, gate_t[...])
        gate_grad = gate_grad + nn(normed_t[half, i], grad_logit)
        out_grad = out_grad + nn(xn, grad_proj[i, lanes, :])
        return gate_grad, out_grad

    zero = jnp.zeros((C, C), F32)
    new = lax.fori_loop(0, ROWS, step, (zero, zero), unroll=4)
    for w in range(2):
        grads[2 + w] = new[w] if half == 0 else grads[2 + w] + new[w]


def grad_of_left(half, group, grad, right, dst):
    def step(c, _):
        dst[half, :, c] = nn(whole(grad, c), plane(right, half, c)).astype(BF16).reshape(DAP, ROWS, 128)
        return 0

    lax.fori_loop(group * GROUP, (group + 1) * GROUP, step, 0, unroll=4)


def grad_of_right(half, group, grad, left, dst):
    def step(c, _):
        dst[half, :, c] = tn(whole(grad, c), plane(left, half, c)).astype(BF16).reshape(DAP, ROWS, 128)
        return 0

    lax.fori_loop(group * GROUP, (group + 1) * GROUP, step, 0, unroll=4)


def unpack(src, w, half, mask, tall):
    m = mask[:, half * 128 : (half + 1) * 128]

    def step(b, _):
        for u in range(SLICE):
            tall[w, half, tile_at(b, u), :] = src[half, b, u].astype(F32) * m
        return 0

    lax.fori_loop(0, DAP, step, 0)


def last_grads(half, w, tall, normed, both, grads):
    lanes = slice(half * 128, (half + 1) * 128)
    rows = slice(w * C, (w + 1) * C)

    def step(p, acc):
        sides = []
        for i in (2 * p, 2 * p + 1):
            sides.append(tall.at[w, half][pl.ds(i, C, stride=PITCH), :].astype(BF16))
            both[i, rows, :] = sides[-1]
        cells = jnp.concatenate([normed[2 * p, lanes, :], normed[2 * p + 1, lanes, :]], axis=0)
        return acc + nn(jnp.concatenate(sides, axis=1), cells)

    acc = lax.fori_loop(0, ROWS // 2, step, jnp.zeros((C, C), F32), unroll=4).T
    grads[w] = acc if half == 0 else grads[w] + acc


def last_pair(half, both, z_hat, z_inv, from_gate, lr, out):
    lanes = slice(half * 128, (half + 1) * 128)

    def step(i, _):
        grad = nn(lr[...], both[i]).T + from_gate[i, lanes, :]
        z = z_hat[i, lanes, :]
        first = jnp.sum(grad, axis=-1, keepdims=True) * (1.0 / C)
        second = jnp.sum(grad * z, axis=-1, keepdims=True) * (1.0 / C)
        out[i, lanes, :] = (z_inv[i, lanes, :] * (grad - first - z * second)).astype(BF16)
        return 0

    lax.fori_loop(0, ROWS, step, 0, unroll=4)


def gram_schmidt(panel):
    lane = lax.broadcasted_iota(jnp.int32, (1, C), 1)
    within = lax.rem(lane, RANK)

    def spread(j):
        return jnp.where(
            lane < RANK,
            jnp.broadcast_to(panel[:, j : j + 1], (C, C)),
            jnp.broadcast_to(panel[:, RANK + j : RANK + j + 1], (C, C)),
        )

    coming = {j: spread(j) for j in range(AHEAD + 1)}
    for j in range(RANK):
        v = coming.pop(j)
        per = 1.0 / jnp.sum(v * v, axis=0, keepdims=True)
        for k in list(coming):
            alpha = jnp.sum(coming[k] * v, axis=0, keepdims=True) * per
            coming[k] = coming[k] - alpha * v
        on_v = jnp.sum(panel * v, axis=0, keepdims=True) * per
        panel = panel - jnp.where(within > j, on_v, 0.0) * v
        if j + AHEAD + 1 < RANK:
            coming[j + AHEAD + 1] = spread(j + AHEAD + 1)
    unit = panel * lax.rsqrt(jnp.sum(panel * panel, axis=0, keepdims=True))
    return jnp.where(lane < 2 * RANK, unit, 0.0)


class Compression:
    def __init__(self, first, refs, grads, error_in, q_init, update, error_out):
        self.first = first
        self.part16, self.got16, self.crop16, self.chunk, self.got32, self.mean, self.send, self.recv = refs
        self.grads, self.error_in, self.q_init = grads, error_in, q_init
        self.update, self.error_out = update, error_out
        self.me, self.dp = lax.axis_index("dap"), lax.axis_index("dp")
        self.mine = pl.ds(pl.multiple_of(self.me * PART, PART), PART)
        self.others = pl.ds(0, 2 * C - PART)
        self.replicas = pl.ds(0, DP - 1)

    def scatter(self):
        for w in range(2):
            self.part16[w * C : (w + 1) * C, :] = self.grads[self.first + w].astype(BF16)
        for t, peer in enumerate(peers()):
            block = self.part16.at[pl.ds(pl.multiple_of(peer * PART, PART), PART)]
            remote(block, self.got16.at[t], self.send.at[0], self.recv.at[0], "dap", peer)

    def across(self):
        await_bytes(self.got16, self.recv.at[0])
        total = self.part16[self.mine, :].astype(F32)
        for t in range(DAP - 1):
            total = total + self.got16[t].astype(F32)
        self.crop16[self.mine, :] = (total * (1.0 / N)).astype(BF16)
        matrix = self.first + self.me // 8
        row = pl.multiple_of(lax.rem(self.me, 8) * PART, PART)
        self.chunk[...] = self.crop16[self.mine, :].astype(F32) + self.error_in[matrix, pl.ds(row, PART), :]
        self.got32[self.dp] = self.chunk[...]
        for s in (4, 5, 3, 6, 2, 7, 1):
            peer = lax.rem(self.dp + s, DP)
            remote(self.chunk, self.got32.at[self.dp], self.send.at[1], self.recv.at[1], "dp", peer)

    def share(self):
        for peer in peers():
            block = self.crop16.at[self.mine]
            remote(block, block, self.send.at[2], self.recv.at[2], "dap", peer)

    def gather(self):
        await_bytes(self.got32.at[self.replicas], self.recv.at[1])
        total = self.got32[0]
        for r in range(1, DP):
            total = total + self.got32[r]
        self.mean[self.mine, :] = total * (1.0 / DP)
        for peer in peers():
            block = self.mean.at[self.mine]
            remote(block, block, self.send.at[3], self.recv.at[3], "dap", peer)

    def finish(self):
        await_bytes(self.mean.at[self.others], self.recv.at[3])
        panel = sum(
            exact(self.mean[w * C : (w + 1) * C, :], self.q_init[self.first + w], 1, 0) for w in range(2)
        )
        basis = gram_schmidt(panel)
        rows = basis.T
        lane = lax.broadcasted_iota(jnp.int32, (1, C), 1)
        await_bytes(self.crop16.at[self.others], self.recv.at[2])
        for w in range(2):
            here = slice(w * C, (w + 1) * C)
            coeffs = exact(rows, self.mean[here, :], 1, 0)
            new = exact(jnp.where(lane // RANK == w, basis, 0.0), coeffs, 1, 0)
            self.update[self.first + w] = new
            memory = self.crop16[here, :].astype(F32) + self.error_in[self.first + w]
            self.error_out[self.first + w] = memory - new

    def sent(self):
        await_bytes(self.part16.at[self.others], self.send.at[0])
        await_bytes(self.got32.at[self.replicas], self.send.at[1])
        await_bytes(self.crop16.at[self.others], self.send.at[2])
        await_bytes(self.mean.at[self.others], self.send.at[3])


def main_kernel(
    pair_in, cot_in, error_at, q_at, residue, weights, out, update, error_out,
    pair, cot, error_in, q_init, q_wide,
    grads, mask, lr_t, lr, gate_t, normed, normed_t, gate, grad_proj, z_hat, z_inv, from_gate,
    h_mean, x_mean, x_inv, tall, both,
    send_l, send_r, left, right, prod, x, send_g, grad, to_l, to_r, got_l, got_r,
    fetch, send, recv, *shared,
):
    size = len(shared) // 2
    late = Compression(0, shared[:size], grads, error_in, q_wide, update, error_out)
    early = Compression(2, shared[size:], grads, error_in, q_wide, update, error_out)
    fetched = []
    for k, (src, dst) in enumerate(
        [
            (pair_in.at[:, pl.ds(0, 128)], pair.at[:, pl.ds(0, 128)]),
            (pair_in.at[:, pl.ds(128, 128)], pair.at[:, pl.ds(128, 128)]),
            (cot_in, cot),
            (error_at, error_in),
            (q_at, q_init),
        ]
    ):
        copy = pltpu.make_async_copy(src, dst, fetch.at[k])
        copy.start()
        fetched.append(copy)
    greet()
    set_up(residue, weights, mask, lr_t, lr, gate_t)
    started = []

    def begin(k, half, group, src, dst):
        exchange(src, dst, half, group, send.at[k], recv.at[k])
        if not group:
            started.append((src, half, k))

    def arrive(k, half, group, dst):
        these = pl.ds(0, SLICE) if group is None else pl.ds(group * GROUP, GROUP)
        await_bytes(dst.at[half, :, these], recv.at[k, half, group or 0])

    sides = [(send_l, left), (send_r, right)]
    for half in range(2):
        fetched[half].wait()
        front(half, pair, lr_t, normed, normed_t, z_hat, z_inv, tall)
        for w, (src, dst) in enumerate(sides):
            pack(tall, w, half, mask, src)
            if half == 0 and w == 0:
                greeted()
            begin(w, half, 0, src, dst)
    for half in range(2):
        for w, (src, dst) in enumerate(sides):
            begin(w, half, 1, src, dst)
    for copy in fetched[2:]:
        copy.wait()
    for w in range(4):
        parts = [q_init[w], jnp.zeros((C - RANK, C), F32)]
        if w % 2:
            parts = [jnp.zeros((RANK, C), F32), q_init[w], jnp.zeros((C - 2 * RANK, C), F32)]
        q_wide[w] = jnp.concatenate(parts, axis=0).T
    for half in range(2):
        gating(half, cot, normed, weights, gate, grad_proj, tall, h_mean)
    for group in range(2):
        for half in range(2):
            for w in range(2):
                arrive(w, half, group, sides[w][1])
        first_triangle(0, group, left, right, prod)
        begin(2, 0, group, prod, x)
    for group in range(2):
        first_triangle(1, group, left, right, prod)
    begin(2, 1, None, prod, x)
    for half in range(2):
        for group in range(2) if half == 0 else [None]:
            arrive(2, half, group, x)
        mid_core(half, x, tall, h_mean, x_mean, x_inv, send_g)
        for group in [None] if half == 0 else range(2):
            begin(3, half, group, send_g, grad)
        mid_rest(
            half, x, x_mean, x_inv, cot, normed_t, gate, grad_proj, weights, gate_t,
            tall, from_gate, grads,
        )
    early.scatter()
    for group in range(2):
        if group == 0:
            arrive(3, 0, None, grad)
        arrive(3, 1, group, grad)
        grad_of_left(0, group, grad, right, to_l)
        begin(4, 0, group, to_l, got_l)
        grad_of_right(0, group, grad, left, to_r)
        begin(5, 0, group, to_r, got_r)
    for group in range(2):
        grad_of_left(1, group, grad, right, to_l)
    begin(4, 1, None, to_l, got_l)
    for group in range(2):
        grad_of_right(1, group, grad, left, to_r)
    begin(5, 1, None, to_r, got_r)
    early.across()
    for half in range(2):
        for w, src in enumerate([got_l, got_r]):
            for group in range(2) if half == 0 else [None]:
                arrive(4 + w, half, group, src)
            unpack(src, w, half, mask, tall)
            last_grads(half, w, tall, normed, both, grads)
        if half == 0:
            last_pair(half, both, z_hat, z_inv, from_gate, lr, out)
    late.scatter()
    early.gather()
    early.share()
    last_pair(1, both, z_hat, z_inv, from_gate, lr, out)
    late.across()
    late.gather()
    late.share()
    early.finish()
    late.finish()
    late.sent()
    early.sent()
    for src, half, k in started:
        await_bytes(src.at[half, pl.ds(0, DAP - 1)], send.at[k, half])


def main_call(*operands):
    vmem = pl.BlockSpec(memory_space=pltpu.VMEM)
    hbm = pl.BlockSpec(memory_space=pl.ANY)
    blocks = pltpu.VMEM((2, DAP, SLICE, ROWS, 128), BF16)
    wide = pltpu.VMEM((ROWS, N, C), F32)
    half_wide = pltpu.VMEM((ROWS, N, C), BF16)
    return pl.pallas_call(
        main_kernel,
        name="triangle",
        out_shape=(
            pltpu.VMEM((ROWS, N, C), BF16),
            pltpu.VMEM((4, C, C), F32),
            pltpu.VMEM((4, C, C), F32),
        ),
        in_specs=[hbm] * 4 + [vmem] * 2,
        out_specs=(vmem, vmem, vmem),
        scratch_shapes=[
            half_wide,
            half_wide,
            pltpu.VMEM((4, C, C), F32),
            pltpu.VMEM((4, RANK, C), F32),
            pltpu.VMEM((4, C, C), F32),
            pltpu.VMEM((4, C, C), F32),
            pltpu.VMEM((ROWS, N), F32),
            pltpu.VMEM((2 * C, C), BF16),
            pltpu.VMEM((C, 2 * C), BF16),
            pltpu.VMEM((C, C), BF16),
            half_wide,
            pltpu.VMEM((2, ROWS, C, 128), BF16),
            wide,
            half_wide,
            wide,
            wide,
            wide,
            pltpu.VMEM((ROWS, N), F32),
            pltpu.VMEM((ROWS, N), F32),
            pltpu.VMEM((ROWS, N), F32),
            pltpu.VMEM((2, 2, C * PITCH, 128), F32),
            pltpu.VMEM((ROWS, 2 * C, 128), BF16),
        ]
        + [blocks] * 12
        + [
            pltpu.SemaphoreType.DMA((5,)),
            pltpu.SemaphoreType.DMA((6, 2)),
            pltpu.SemaphoreType.DMA((6, 2, 2)),
        ]
        + [
            pltpu.VMEM((2 * C, C), BF16),
            pltpu.VMEM((DAP - 1, PART, C), BF16),
            pltpu.VMEM((2 * C, C), BF16),
            pltpu.VMEM((PART, C), F32),
            pltpu.VMEM((DP, PART, C), F32),
            pltpu.VMEM((2 * C, C), F32),
            pltpu.SemaphoreType.DMA((4,)),
            pltpu.SemaphoreType.DMA((4,)),
        ]
        * 2,
        compiler_params=pltpu.CompilerParams(
            collective_id=0, has_side_effects=True, vmem_limit_bytes=56 << 20
        ),
    )(*operands)


def store_kernel(*refs):
    sources, targets, sems = refs[:3], refs[3:6], refs[6]
    copies = [
        pltpu.make_async_copy(src, dst, sems.at[k])
        for k, (src, dst) in enumerate(zip(sources, targets))
    ]
    for copy in copies:
        copy.start()
    for copy in copies:
        copy.wait()


def store(*arrays):
    vmem = pl.BlockSpec(memory_space=pltpu.VMEM)
    hbm = pl.BlockSpec(memory_space=pl.ANY)
    return pl.pallas_call(
        store_kernel,
        name="store",
        out_shape=tuple(jax.ShapeDtypeStruct(a.shape, a.dtype) for a in arrays),
        in_specs=[vmem] * 3,
        out_specs=(hbm,) * 3,
        scratch_shapes=[pltpu.SemaphoreType.DMA((3,))],
        compiler_params=pltpu.CompilerParams(vmem_limit_bytes=8 << 20),
    )(*arrays)


def per_device(pair_act, cotangent, residue_mask, weights, error_in, q_init):
    results = main_call(
        pair_act[0], cotangent[0], error_in[0], q_init.transpose(0, 2, 1), residue_mask, weights
    )
    grad_pair, update, error_out = store(*results)
    return (grad_pair[None], update, error_out[None])


def solution(mesh):
    placed = (
        P("dp", "dap", None, None),
        P("dp", "dap", None, None),
        P("dp", None),
        P(),
        P("dp", None, None, None),
        P(),
    )
    return jax.shard_map(
        per_device,
        mesh=mesh,
        in_specs=placed,
        out_specs=(P("dp", "dap", None, None), P(), P("dp", None, None, None)),
        check_vma=False,
    )
```
